512 devices in a mesh: dp: 4 (over x), expert: 128 (over y, z, core).
Axes of the slice: x: 4, y: 8, z: 8, core: 2. Of those that a mesh axis runs over, the one named last changes fastest.
Arguments:
- embeds: bfloat16 [3, 2048, 1024], P(None, 'expert', 'dp'), may hold values from -6 to 6
- prefix_cache: bfloat16 [2048, 2, 64, 1024], P('expert', None, None, 'dp'), may hold values from -6 to 6
- w_qkv: bfloat16 [1024, 3, 1024], P(None, None, 'dp'), may hold values from -0.1875 to 0.1875
- w_up: bfloat16 [128, 1024, 2048], P('expert', None, 'dp'), may hold values from -0.1875 to 0.1875
- w_down: bfloat16 [128, 2048, 1024], P('expert', 'dp'), may hold values from -0.09375 to 0.09375
- parents: int32 [3, 2048], P(None, 'expert'), may hold values from 0 to 7
- routes: int32 [3, 2048, 2], P(None, 'expert'), may hold values from 0 to 63, all different within a row; in each aligned block of 16 rows (0 to 15, 16 to 31, ..., all dimensions but the last counted through in order) at most 2 rows name the same one
- gates: float32 [3, 2048, 2], P(None, 'expert'), may hold values from 0.2 to 1
Outputs:
- mixed: bfloat16 [3, 2048, 1024], P(None, 'expert', 'dp')
The draws below stay inside these ranges and needn't reach their ends.
Inputs may be any that keep to these rules, and one draw needn't show every extreme that they name: `routes`: at each step the 16 rows of one device name one expert at most 2 times.
All inputs are finite; a program needn't handle non-finite values.
Results may differ from the reference program's by a relative error of at most 0.011.
Values may be sent and summed in bfloat16 or wider, within the bound.
No kernel may reach another device: no remote copies, remote signals or barrier semaphores. Data moves between devices by JAX's collectives and lax.ppermute only.
A program may use at most 64 MiB of HBM per device.

```python
import math
import jax
import jax.numpy as jnp
import numpy as np
from jax import lax

D = 1024
HD = 128
HEADS = 8
FF = 4096
HALVES = 2
BEAMS = 8
PREFIX = 64
STEPS = 3
R_DEV = 16
EXPERTS = 64
ROWS = 2048
CAP_E = 2
N_EXPERT = 128


def place_ends(values, key, low, high):
    spot = [jax.random.randint(jax.random.fold_in(key, axis), (), 0, length) for axis, length in enumerate(values.shape)]
    widest = values.shape.index(max(values.shape))
    neighbour = spot[:widest] + [(spot[widest] + 1) % values.shape[widest]] + spot[widest + 1:]
    return values.at[tuple(spot)].set(low).at[tuple(neighbour)].set(high)


def levels(key, shape, shards, low, high):
    level, own = 1.0, jax.random.fold_in(key, 6)
    for axis_at, parts in shards:
        steps = jnp.exp(jax.random.uniform(jax.random.fold_in(own, axis_at), (parts,), jnp.float32, low / len(shards), high / len(shards)))
        level = level * jnp.repeat(steps, shape[axis_at] // parts).reshape([-1 if axis == axis_at else 1 for axis in range(len(shape))])
    return level


def rank_table(number_of, skew):
    portions = [(1 << 20) // math.isqrt(rank ** skew) + 1 for rank in range(1, number_of + 1)]
    width = 1 + sum(portions) // (1 << 30)
    return np.cumsum(np.array([max(1, weight // width) for weight in portions]))


def ranked_ids(rng, dims, number_of, slope):
    table = rank_table(number_of, slope)
    pick = jax.random.randint(jax.random.fold_in(rng, 1), dims, 0, int(table[number_of - 1]))
    grade = jnp.searchsorted(jnp.asarray(table, jnp.int32), pick, side="right")
    return jax.random.permutation(jax.random.fold_in(rng, 2), number_of)[grade].astype(jnp.int32)


def assign_block(stream_key, own, number, rows, number_of, top, most, lean):
    order = jax.random.permutation(stream_key, number_of)
    heavy_load, ordinary = load_shares(number_of, rows * top, most, lean, True), load_shares(number_of, rows * top, most, lean, False)
    places = jnp.arange(number_of)

    def named(sizes, offset_by):
        used = int((sizes > 0).sum())
        fixed = max(1, used // 4)
        shifted = fixed + (places - fixed + offset_by * (used - fixed)) % max(1, number_of - fixed)
        return jnp.zeros((number_of,), jnp.int32).at[order[jnp.where(places < fixed, places, shifted)]].set(jnp.asarray(sizes, jnp.int32))

    sizes = jnp.where(number % 4 == 0, named(heavy_load, number // 4), named(ordinary, number - number // 4 - 1))
    mixed = jax.random.permutation(jax.random.fold_in(own, 3), number_of)
    giver, taker = mixed[0:number_of // 2 * 2:2], mixed[1:number_of // 2 * 2:2]
    room = jnp.minimum(sizes[giver] - 1, most - sizes[taker]) // 2
    room = jnp.where((giver == order[0]) | (taker == order[0]) | (sizes[taker] == 0), 0, jnp.maximum(room, 0))
    shifted = jax.random.randint(jax.random.fold_in(own, 4), (number_of // 2,), 0, 1 << 20) % (room + 1)
    sizes = sizes.at[giver].add(-shifted).at[taker].add(shifted)
    members = jnp.searchsorted(jnp.cumsum(sizes), jnp.arange(rows * top), side="right").astype(jnp.int32)
    listing = members.reshape(top, rows).T
    listing = listing[jax.random.permutation(jax.random.fold_in(own, 1), rows)]
    offset_by = jax.random.randint(jax.random.fold_in(own, 2), (rows, 1), 0, top)
    return jnp.take_along_axis(listing, (jnp.arange(top)[None, :] + offset_by) % top, axis=1)


def load_shares(count, total, reach, skew, full):
    portions = [(1 << 20) // math.isqrt(rank ** skew) + 1 for rank in range(1, count + 1)]
    largest = reach if full else min(reach, max(-(-total // count), total * portions[0] // sum(portions)))
    least = 1 if total - largest >= count - 1 else 0
    given, surplus = [largest] + [least] * (count - 1), total - largest - least * (count - 1)
    while surplus > 0:
        movable = [i for i in range(1, count) if given[i] < largest] or [i for i in range(1, count) if given[i] < reach]
        mass, remaining = sum([portions[i] for i in movable]), surplus
        for i in movable:
            addition = min(reach - given[i], max(1, remaining * portions[i] // mass), surplus)
            given[i] = given[i] + addition
            surplus = surplus - addition
    return np.array(given)


def gaussian(key, extent, scale, limit, split=(), kind=jnp.bfloat16):
    array = scale * jax.random.normal(key, extent, jnp.float32)
    if split:
        array = array * levels(key, extent, split, -0.22, 0.18)
    return jnp.clip(array, -limit, limit).astype(kind)


def setup_inputs(seed: int = 0) -> dict:
    splits = jax.random.split(jax.random.key(seed), 9)
    embeds = gaussian(splits[0], (STEPS, ROWS, D), 1.0, 6.0, ((1, 128), (2, 4)))
    prefix_cache = gaussian(splits[1], (ROWS, 2, PREFIX, D), 1.0, 6.0, ((0, 128), (3, 4)))
    w_qkv = gaussian(splits[2], (D, 3, D), D ** -0.5, 0.1875, ((2, 4),))
    w_up = gaussian(splits[3], (EXPERTS * HALVES, D, FF // HALVES), D ** -0.5, 0.1875, ((0, 128), (2, 4)))
    w_down = gaussian(splits[4], (EXPERTS * HALVES, FF // HALVES, D), FF ** -0.5, 0.09375, ((0, 128), (1, 4)))
    parents = place_ends(ranked_ids(splits[5], (STEPS, ROWS), BEAMS, 2), jax.random.fold_in(splits[5], 3), 0, BEAMS - 1).astype(jnp.int32)
    routes_keys = jax.random.split(jax.random.fold_in(splits[6], 1), STEPS * ROWS // R_DEV)
    routes_turns = jax.random.permutation(jax.random.fold_in(splits[6], 3), STEPS * ROWS // R_DEV)
    routes = jax.vmap(lambda own, number: assign_block(jax.random.fold_in(splits[6], 2), own, number, R_DEV, EXPERTS, 2, CAP_E, 2))(routes_keys, routes_turns).reshape((STEPS, ROWS, 2))
    gates = jnp.clip(0.2 + 0.8 * jax.random.uniform(splits[7], (STEPS, ROWS, 2), jnp.float32) ** levels(splits[7], (STEPS, ROWS, 2), ((1, 128),), -0.2, 0.2), 0.2, 1.0)
    return {"embeds": embeds, "prefix_cache": prefix_cache, "w_qkv": w_qkv, "w_up": w_up, "w_down": w_down, "parents": parents, "routes": routes, "gates": gates}


def normalize(values):
    mean_value = lax.optimization_barrier(jnp.mean(values, axis=-1, keepdims=True))
    centred = values - mean_value
    spread = lax.optimization_barrier(jnp.mean(centred * centred, axis=-1, keepdims=True))
    return centred * lax.rsqrt(spread + 1e-05)

def attend_all(query, history, visible):
    length = history.shape[2]
    query_heads = query.reshape(ROWS, HEADS, HD).astype(jnp.float32).transpose(1, 0, 2)
    key_heads = history[:, 0].reshape(ROWS, length, HEADS, HD).transpose(2, 0, 1, 3)
    value_heads = history[:, 1].reshape(ROWS, length, HEADS, HD).transpose(2, 0, 1, 3)
    shown = jnp.arange(length) < visible

    def one_head(inputs):
        query_one, key_one, value_one = inputs
        scores = jnp.einsum('rd,rld->rl', query_one, key_one.astype(jnp.float32), precision=lax.Precision.HIGHEST) * HD ** (-0.5)
        weights = jnp.where(shown[None, :], jnp.exp(scores), jnp.float32(0.0))
        total = lax.optimization_barrier(jnp.sum(weights, axis=-1))
        summed = jnp.einsum('rl,rld->rd', weights, value_one.astype(jnp.float32), precision=lax.Precision.HIGHEST)
        return summed / total[:, None]
    heads_out = lax.map(one_head, (query_heads, key_heads, value_heads))
    return heads_out.transpose(1, 0, 2).reshape(ROWS, D)

def experts_ref(middle, route, gate, up_pairs, down_pairs):
    normed = normalize(middle.astype(jnp.float32)).astype(jnp.bfloat16)
    flat_expert = route.reshape(-1).astype(jnp.int32)
    flat_row = (jnp.arange(2 * ROWS) // 2).astype(jnp.int32)
    flat_gate = gate.reshape(-1)
    most = N_EXPERT * CAP_E

    def one_expert(accum, inputs):
        up_half, down_half, index = inputs
        key_order = (flat_expert != index).astype(jnp.int32)
        order = jnp.argsort(key_order, stable=True)[:most].astype(jnp.int32)
        valid = flat_expert[order] == index
        chosen_rows = flat_row[order]
        picked = normed[chosen_rows]
        expert_out = jnp.zeros((most, D), jnp.float32)
        for half in range(HALVES):
            hidden = jax.nn.relu(jnp.dot(picked, up_half[half], preferred_element_type=jnp.float32)).astype(jnp.bfloat16)
            piece = jnp.dot(hidden, down_half[half], preferred_element_type=jnp.float32).astype(jnp.bfloat16)
            piece = lax.optimization_barrier(piece)
            expert_out = expert_out + piece.astype(jnp.float32)
        contrib = jnp.where(valid, flat_gate[order], jnp.float32(0.0))[:, None] * expert_out
        return (accum.at[chosen_rows].add(contrib), index)
    accum = lax.scan(one_expert, jnp.zeros((ROWS, D), jnp.float32), (up_pairs, down_pairs, jnp.arange(EXPERTS, dtype=jnp.int32)))[0]
    return (middle.astype(jnp.float32) + accum).astype(jnp.bfloat16)

def reference(embeds, prefix_cache, w_qkv, w_up, w_down, parents, routes, gates):
    rows = jnp.arange(ROWS, dtype=jnp.int32)
    first_beam = rows - rows % BEAMS
    history = jnp.concatenate([prefix_cache, jnp.zeros((ROWS, 2, STEPS, D), jnp.bfloat16)], axis=2)
    joined = w_qkv.reshape(D, 3 * D)
    up_pairs = w_up.reshape(EXPERTS, HALVES, D, FF // HALVES)
    down_pairs = w_down.reshape(EXPERTS, HALVES, FF // HALVES, D)
    results = []
    for step in range(STEPS):
        source = (first_beam + parents[step]).astype(jnp.int32)
        history = jnp.take(history, source, axis=0)
        token = embeds[step]
        normed = normalize(token.astype(jnp.float32)).astype(jnp.bfloat16)
        projected = jnp.dot(normed, joined, preferred_element_type=jnp.float32).astype(jnp.bfloat16).reshape(ROWS, 3, D)
        history = history.at[:, :, PREFIX + step].set(projected[:, 1:])
        attention = attend_all(projected[:, 0], history, PREFIX + step + 1)
        middle = (token.astype(jnp.float32) + attention).astype(jnp.bfloat16)
        results.append(experts_ref(middle, routes[step], gates[step], up_pairs, down_pairs))
    return jnp.stack(results)
```

```python
import functools

import jax
import jax.numpy as jnp
from jax import lax
from jax.experimental import pallas as pl
from jax.experimental.pallas import tpu as pltpu
from jax.sharding import Mesh
from jax.sharding import PartitionSpec as P

HD = 128
CORES = 2
BEAMS = 8
CAP = 2
PAD = 8
HIDE = -1e30
F32 = jnp.float32
BF16 = jnp.bfloat16


def iota(shape, dim):
    return lax.broadcasted_iota(jnp.int32, shape, dim)


def dot(a, b):
    return jnp.dot(a, b, preferred_element_type=F32)


def dot_last(a, b):
    return lax.dot_general(a, b, (((1,), (1,)), ((), ())), preferred_element_type=F32)


def call(kernel, outs, *args, cost=None):
    flops, nbytes = cost or (0, 0)
    return pl.pallas_call(
        kernel,
        out_shape=outs,
        in_specs=[pl.BlockSpec(memory_space=pltpu.VMEM)] * len(args),
        out_specs=jax.tree.map(lambda _: pl.BlockSpec(memory_space=pltpu.VMEM), outs),
        compiler_params=pltpu.CompilerParams(vmem_limit_bytes=32 * 1024 * 1024),
        cost_estimate=pl.CostEstimate(flops=flops, bytes_accessed=nbytes, transcendentals=0),
    )(*args)


def plan_kernel(rows, steps, prefix, experts, parents_ref, route_row_ref, route_col_ref, gate_ref, bias_ref, pack_ref, high_ref, low_ref):
    total = rows * steps
    local = iota((rows, 1), 0)
    first = local - local % BEAMS
    parent = [
        (iota((rows, rows), 1) == first + parents_ref[t * rows : (t + 1) * rows, :]).astype(F32).astype(BF16)
        for t in range(steps)
    ]
    eye = (iota((rows, rows), 0) == iota((rows, rows), 1)).astype(F32)
    none = jnp.zeros((rows, rows), F32)
    origin = []
    seen = []
    for t in range(steps):
        if t == 0:
            origin.append(parent[0].astype(F32))
            seen.append([eye] + [none] * (steps - 1))
        else:
            origin.append(dot(parent[t], origin[t - 1].astype(BF16)))
            seen.append([dot(parent[t], seen[t - 1][s].astype(BF16)) for s in range(t)] + [eye] + [none] * (steps - 1 - t))
    spread = (iota((rows, rows * prefix), 1) // prefix == iota((rows, rows * prefix), 0)).astype(F32).astype(BF16)
    old = dot(jnp.concatenate(origin, axis=0).astype(BF16), spread)
    bias_ref[:, : rows * prefix] = jnp.where(old > 0.5, 0.0, HIDE)
    new = jnp.concatenate([jnp.concatenate(seen[t], axis=1) for t in range(steps)], axis=0)
    bias_ref[:, rows * prefix :] = jnp.full((total, HD), HIDE, F32)
    bias_ref[:, rows * prefix : rows * prefix + total] = jnp.where(new > 0.5, 0.0, HIDE)

    a, b = iota((total, total), 0), iota((total, total), 1)
    same = a // rows == b // rows
    before = (same & (b < a)).astype(F32).astype(BF16)
    after = (same & (a < b)).astype(F32).astype(BF16)
    named = [(iota((total, experts), 1) == route_col_ref[:, k : k + 1]).astype(F32) for k in range(2)]
    count = dot(before, (named[0] + named[1]).astype(BF16))
    step_at = (iota((total, 1), 0) // rows) * CAP
    weights = jnp.zeros((total, experts * PAD), F32)
    for k in range(2):
        order = jnp.sum(named[k] * count, axis=1, keepdims=True).astype(jnp.int32)
        target = route_col_ref[:, k : k + 1] * PAD + step_at + order
        weights += jnp.where(iota((total, experts * PAD), 1) == target, gate_ref[:, k : k + 1], 0.0)
    high = weights.astype(BF16)
    high_ref[...] = high
    low_ref[...] = (weights - high.astype(F32)).astype(BF16)

    named = [(iota((experts, total), 0) == route_row_ref[k : k + 1, :]).astype(F32) for k in range(2)]
    count = dot((named[0] + named[1]).astype(BF16), after)
    step_at = (iota((1, total), 1) // rows) * CAP
    chosen = jnp.zeros((experts * PAD, total), F32)
    for k in range(2):
        order = jnp.sum(named[k] * count, axis=0, keepdims=True).astype(jnp.int32)
        target = route_row_ref[k : k + 1, :] * PAD + step_at + order
        chosen += (iota((experts * PAD, total), 0) == target).astype(F32)
    pack_ref[...] = chosen.astype(BF16)


def normed_blocks(blocks):
    width = sum(v.shape[-1] for v in blocks)
    mean = sum(jnp.sum(v, axis=-1, keepdims=True) for v in blocks) / width
    centred = [v - mean for v in blocks]
    spread = sum(jnp.sum(v * v, axis=-1, keepdims=True) for v in centred) / width
    scale = lax.rsqrt(spread + 1e-05)
    return jnp.concatenate([(v * scale).astype(BF16) for v in centred], axis=-1)


def attend_kernel(prefix, gathered_ref, token_ref, w_ref, cache_ref, bias_ref, pack_ref, middle_ref, packed_ref):
    parts = gathered_ref.shape[0]
    total, shard = token_ref.shape
    rows = cache_ref.shape[0]
    normed = normed_blocks([gathered_ref[i].astype(F32) for i in range(parts)])
    query, key, value = (dot(normed, w_ref[j]).astype(BF16) for j in range(3))
    bias_old = bias_ref[:, : rows * prefix]
    bias_new = bias_ref[:, rows * prefix : rows * prefix + total]
    for h in range(shard // HD):
        at = slice(h * HD, (h + 1) * HD)
        old_keys = cache_ref[:, 0, :, at].reshape(rows * prefix, HD)
        old_values = cache_ref[:, 1, :, at].reshape(rows * prefix, HD)
        w_old = jnp.exp(dot_last(query[:, at], old_keys) * HD ** (-0.5) + bias_old)
        w_new = jnp.exp(dot_last(query[:, at], key[:, at]) * HD ** (-0.5) + bias_new)
        weight = jnp.sum(w_old, axis=-1, keepdims=True) + jnp.sum(w_new, axis=-1, keepdims=True)
        summed = dot(w_old.astype(BF16), old_values) + dot(w_new.astype(BF16), value[:, at])
        middle_ref[:, at] = (token_ref[:, at].astype(F32) + summed / weight).astype(BF16)
    packed_ref[...] = dot(pack_ref[...], middle_ref[...]).astype(BF16)


def spread_kernel(used, arrived_ref, out_ref):
    group = 8
    keep = (iota((group * used, group * PAD), 1) == (iota((group * used, 1), 0) // used) * PAD + iota((group * used, 1), 0) % used)
    keep = keep.astype(F32).astype(BF16)
    for g in range(arrived_ref.shape[0] // (group * PAD)):
        block = dot(keep, arrived_ref[g * group * PAD : (g + 1) * group * PAD, :]).astype(BF16)
        for i in range(out_ref.shape[0]):
            out_ref[i, g * group * used : (g + 1) * group * used, :] = block


def expert_kernel(slots_ref, up_ref, up_other_ref, down_ref, down_other_ref, out_ref):
    parts, slots, shard = slots_ref.shape
    block = slots // 3
    for g in range(slots // block):
        at = slice(g * block, (g + 1) * block)
        normed = normed_blocks([slots_ref[i, at, :].astype(F32) for i in range(parts)])
        hidden = jax.nn.relu(dot(normed, up_ref[0])).astype(BF16)
        hidden_other = jax.nn.relu(dot(normed, up_other_ref[0])).astype(BF16)
        piece = dot(hidden, down_ref[0]) + dot(hidden_other, down_other_ref[0])
        for i in range(parts):
            out_ref[i, at, :] = piece[:, i * shard : (i + 1) * shard].astype(BF16)


def sum_kernel(used, parts_ref, out_ref):
    group = 8
    place = (iota((group * PAD, group * used), 0) == (iota((1, group * used), 1) // used) * PAD + iota((1, group * used), 1) % used)
    place = place.astype(F32).astype(BF16)
    for g in range(out_ref.shape[0] // (group * PAD)):
        at = slice(g * group * used, (g + 1) * group * used)
        total = sum(parts_ref[i, at, :].astype(F32) for i in range(parts_ref.shape[0]))
        out_ref[g * group * PAD : (g + 1) * group * PAD, :] = dot(place, total.astype(BF16)).astype(BF16)


def combine_kernel(middle_ref, returned_ref, high_ref, low_ref, out_ref):
    returned = returned_ref[...]
    added = dot(high_ref[...], returned) + dot(low_ref[...], returned)
    out_ref[...] = (middle_ref[...].astype(F32) + added).astype(BF16)


def shards(parts, experts, embeds, prefix_cache, w_qkv, w_up, w_down, parents, routes, gates):
    steps, rows, shard = embeds.shape
    width = w_qkv.shape[0]
    prefix = prefix_cache.shape[2]
    total = steps * rows
    used = steps * CAP
    slots = experts * used
    shape = jax.ShapeDtypeStruct

    def exchange(values, axis):
        return lax.all_to_all(values, axis, split_axis=0, concat_axis=0, tiled=True)

    tokens = embeds.reshape(total, shard)
    gathered = exchange(jnp.broadcast_to(tokens[None], (parts, total, shard)), "x")
    swap = [(i, (i + 1) % CORES) for i in range(CORES)]
    up_other = lax.ppermute(w_up, "core", swap)
    down_other = lax.ppermute(w_down, "core", swap)
    bias, pack, high, low = call(
        functools.partial(plan_kernel, rows, steps, prefix, experts),
        (
            shape((total, rows * prefix + HD), F32),
            shape((experts * PAD, total), BF16),
            shape((total, experts * PAD), BF16),
            shape((total, experts * PAD), BF16),
        ),
        parents.reshape(total, 1),
        routes.transpose(2, 0, 1).reshape(2, total),
        routes.reshape(total, 2),
        gates.reshape(total, 2),
        cost=(10**8, 10**6),
    )
    middle, packed = call(
        functools.partial(attend_kernel, prefix),
        (shape((total, shard), BF16), shape((experts * PAD, shard), BF16)),
        gathered,
        tokens,
        w_qkv.transpose(1, 0, 2),
        prefix_cache,
        bias,
        pack,
        cost=(2 * total * width * 3 * shard, 3 * 10**6),
    )
    arrived = exchange(packed.reshape(experts, PAD, shard), "yz").reshape(experts * PAD, shard)
    spread = call(functools.partial(spread_kernel, used), shape((parts, slots, shard), BF16), arrived)
    whole = exchange(spread, "x")
    share = call(
        expert_kernel,
        shape((parts, slots, shard), BF16),
        whole,
        w_up,
        up_other,
        w_down,
        down_other,
        cost=(8 * slots * width * w_up.shape[2], 6 * 10**6),
    )
    pieces = exchange(share, "x")
    summed = call(functools.partial(sum_kernel, used), shape((experts * PAD, shard), BF16), pieces)
    returned = exchange(summed.reshape(experts, PAD, shard), "yz").reshape(experts * PAD, shard)
    mixed = call(combine_kernel, shape((total, shard), BF16), middle, returned, high, low)
    return mixed.reshape(steps, rows, shard)


def solution(mesh):
    parts, devices = mesh.shape["dp"], mesh.shape["expert"]
    experts = devices // CORES
    split = Mesh(mesh.devices.reshape(parts, experts, CORES), ("x", "yz", "core"))
    rows = ("yz", "core")
    placed = (
        P(None, rows, "x"),
        P(rows, None, None, "x"),
        P(None, None, "x"),
        P(rows, None, "x"),
        P(rows, "x", None),
        P(None, rows),
        P(None, rows, None),
        P(None, rows, None),
    )
    return jax.shard_map(
        functools.partial(shards, parts, experts), mesh=split, in_specs=placed, out_specs=P(None, rows, "x"), check_vma=False
    )
```

```python
import functools

import jax
import jax.numpy as jnp
from jax import lax
from jax.experimental import pallas as pl
from jax.experimental.pallas import tpu as pltpu
from jax.sharding import Mesh
from jax.sharding import PartitionSpec as P

HD = 128
CORES = 2
BEAMS = 8
CAP = 2
PAD = 8
HIDE = -1e30
F32 = jnp.float32
BF16 = jnp.bfloat16


def iota(shape, dim):
    return lax.broadcasted_iota(jnp.int32, shape, dim)


def dot(a, b):
    return jnp.dot(a, b, preferred_element_type=F32)


def dot_last(a, b):
    return lax.dot_general(a, b, (((1,), (1,)), ((), ())), preferred_element_type=F32)


def call(kernel, outs, *args, cost=None, in_hbm=(), scratch=()):
    flops, nbytes = cost or (0, 0)
    return pl.pallas_call(
        kernel,
        out_shape=outs,
        in_specs=[pl.BlockSpec(memory_space=pl.ANY if i in in_hbm else pltpu.VMEM) for i in range(len(args))],
        out_specs=jax.tree.map(lambda _: pl.BlockSpec(memory_space=pltpu.VMEM), outs),
        scratch_shapes=scratch,
        compiler_params=pltpu.CompilerParams(vmem_limit_bytes=16 * 1024 * 1024),
        cost_estimate=pl.CostEstimate(flops=flops, bytes_accessed=nbytes, transcendentals=0),
    )(*args)


def plan_kernel(
    rows, steps, prefix, experts, first_expert,
    parents_ref, route_ref, gate_ref, w_hbm, cache_hbm, up_hbm, down_hbm,
    bias_ref, pack_ref, high_ref, low_ref, w_ref, cache_ref, expert_ref, sems,
):
    half = up_hbm.shape[1] // 2
    hidden = up_hbm.shape[2]
    copies = [
        pltpu.make_async_copy(up_hbm.at[0, :half, :], expert_ref.at[:, :hidden], sems.at[0]),
        pltpu.make_async_copy(up_hbm.at[0, half:, :], expert_ref.at[:, hidden : 2 * hidden], sems.at[1]),
        pltpu.make_async_copy(down_hbm.at[0], expert_ref.at[:, 2 * hidden :], sems.at[2]),
        pltpu.make_async_copy(w_hbm, w_ref, sems.at[3]),
        pltpu.make_async_copy(cache_hbm, cache_ref, sems.at[4]),
    ]
    for copy in copies:
        copy.start()
    total = rows * steps
    first = iota((rows, 1), 0) // BEAMS * BEAMS
    diagonal = iota((rows, rows), 0) == iota((rows, rows), 1)
    eye = diagonal.astype(F32)

    def column(row):
        return jnp.sum(jnp.where(iota((row.shape[1], row.shape[1]), 0) == iota((row.shape[1], row.shape[1]), 1), row, 0.0), axis=1, keepdims=True)

    parent = [
        (iota((rows, rows), 1) == first + column(parents_ref[t : t + 1, :].astype(F32)).astype(jnp.int32)).astype(F32).astype(BF16)
        for t in range(steps)
    ]
    none = jnp.zeros((rows, rows), F32)
    origin = []
    seen = []
    for t in range(steps):
        if t == 0:
            origin.append(parent[0].astype(F32))
            seen.append([eye] + [none] * (steps - 1))
        else:
            origin.append(dot(parent[t], origin[t - 1].astype(BF16)))
            seen.append([dot(parent[t], seen[t - 1][s].astype(BF16)) for s in range(t)] + [eye] + [none] * (steps - 1 - t))
    spread = (iota((rows, rows * prefix), 1) // prefix == iota((rows, rows * prefix), 0)).astype(F32).astype(BF16)
    old = dot(jnp.concatenate(origin, axis=0).astype(BF16), spread)
    bias_ref[:, : rows * prefix] = jnp.where(old > 0.5, 0.0, HIDE)
    new = jnp.concatenate([jnp.concatenate(seen[t], axis=1) for t in range(steps)], axis=0)
    bias_ref[:, rows * prefix :] = jnp.full((total, HD), HIDE, F32)
    bias_ref[:, rows * prefix : rows * prefix + total] = jnp.where(new > 0.5, 0.0, HIDE)

    a, b = iota((total, total), 0), iota((total, total), 1)
    same = a // rows == b // rows
    after = (same & (a < b)).astype(F32).astype(BF16)
    places = [
        jnp.concatenate([(route_ref[t, k : k + 1, :] + (experts - first_expert)) % experts for t in range(steps)], axis=1)
        for k in range(2)
    ]
    gates = [jnp.concatenate([gate_ref[t, k : k + 1, :] for t in range(steps)], axis=1) for k in range(2)]
    named = [(iota((experts, total), 0) == places[k]).astype(F32) for k in range(2)]
    count = dot((named[0] + named[1]).astype(BF16), after)
    step_at = (iota((1, total), 1) // rows) * CAP
    chosen = jnp.zeros((experts * PAD, total), F32)
    weights = jnp.zeros((total, experts * PAD), F32)
    for k in range(2):
        order = jnp.sum(named[k] * count, axis=0, keepdims=True).astype(jnp.int32)
        target = places[k] * PAD + step_at + order
        chosen += (iota((experts * PAD, total), 0) == target).astype(F32)
        at = column(target.astype(F32)).astype(jnp.int32)
        weights += jnp.where(iota((total, experts * PAD), 1) == at, column(gates[k]), 0.0)
    pack_ref[...] = chosen.astype(BF16)
    high = weights.astype(BF16)
    high_ref[...] = high
    low_ref[...] = (weights - high.astype(F32)).astype(BF16)
    for copy in copies:
        copy.wait()


def normed_blocks(blocks):
    width = sum(v.shape[-1] for v in blocks)
    mean = sum(jnp.sum(v, axis=-1, keepdims=True) for v in blocks) / width
    centred = [v - mean for v in blocks]
    spread = sum(jnp.sum(v * v, axis=-1, keepdims=True) for v in centred) / width
    scale = lax.rsqrt(spread + 1e-05)
    return jnp.concatenate([(v * scale).astype(BF16) for v in centred], axis=-1)


def attend_kernel(prefix, gathered_ref, token_ref, w_ref, cache_ref, bias_ref, pack_ref, middle_ref, packed_ref):
    parts = gathered_ref.shape[0]
    total, shard = token_ref.shape
    rows = cache_ref.shape[0]
    normed = normed_blocks([gathered_ref[i].astype(F32) for i in range(parts)])
    query, key, value = (dot(normed, w_ref[j]).astype(BF16) for j in range(3))
    bias_old = bias_ref[:, : rows * prefix]
    bias_new = bias_ref[:, rows * prefix : rows * prefix + total]
    for h in range(shard // HD):
        at = slice(h * HD, (h + 1) * HD)
        old_keys = cache_ref[:, 0, :, at].reshape(rows * prefix, HD)
        old_values = cache_ref[:, 1, :, at].reshape(rows * prefix, HD)
        w_old = jnp.exp(dot_last(query[:, at], old_keys) * HD ** (-0.5) + bias_old)
        w_new = jnp.exp(dot_last(query[:, at], key[:, at]) * HD ** (-0.5) + bias_new)
        weight = jnp.sum(w_old, axis=-1, keepdims=True) + jnp.sum(w_new, axis=-1, keepdims=True)
        summed = dot(w_old.astype(BF16), old_values) + dot(w_new.astype(BF16), value[:, at])
        middle_ref[:, at] = (token_ref[:, at].astype(F32) + summed / weight).astype(BF16)
    packed_ref[...] = dot(pack_ref[...], middle_ref[...]).astype(BF16)


def spread_kernel(used, arrived_ref, out_ref):
    group = 8
    keep = (iota((group * used, group * PAD), 1) == (iota((group * used, 1), 0) // used) * PAD + iota((group * used, 1), 0) % used)
    keep = keep.astype(F32).astype(BF16)
    for g in range(arrived_ref.shape[0] // (group * PAD)):
        block = dot(keep, arrived_ref[g * group * PAD : (g + 1) * group * PAD, :]).astype(BF16)
        for i in range(out_ref.shape[0]):
            out_ref[i, g * group * used : (g + 1) * group * used, :] = block


def expert_kernel(slots_ref, own_ref, other_ref, out_ref, normed_ref, hidden_ref):
    parts, slots, shard = slots_ref.shape
    half = own_ref.shape[0]
    units = half
    block = slots // 3
    for g in range(slots // block):
        at = slice(g * block, (g + 1) * block)
        normed_ref[at, :] = normed_blocks([slots_ref[i, at, :].astype(F32) for i in range(parts)])
    wide = 256
    for j, ref in enumerate((own_ref, other_ref)):
        for n in range(0, units, wide):
            up = dot(normed_ref[:, :half], ref[:, n : n + wide]) + dot(normed_ref[:, half:], ref[:, units + n : units + n + wide])
            hidden_ref[:, j * units + n : j * units + n + wide] = jax.nn.relu(up).astype(BF16)
    for i in range(parts):
        at = slice(2 * units + i * shard, 2 * units + (i + 1) * shard)
        piece = dot(hidden_ref[:, :units], own_ref[:, at]) + dot(hidden_ref[:, units:], other_ref[:, at])
        out_ref[i] = piece.astype(BF16)


def sum_kernel(used, parts_ref, out_ref):
    group = 8
    place = (iota((group * PAD, group * used), 0) == (iota((1, group * used), 1) // used) * PAD + iota((1, group * used), 1) % used)
    place = place.astype(F32).astype(BF16)
    for g in range(out_ref.shape[0] // (group * PAD)):
        at = slice(g * group * used, (g + 1) * group * used)
        total = sum(parts_ref[i, at, :].astype(F32) for i in range(parts_ref.shape[0]))
        out_ref[g * group * PAD : (g + 1) * group * PAD, :] = dot(place, total.astype(BF16)).astype(BF16)


def combine_kernel(middle_ref, returned_ref, high_ref, low_ref, out_ref):
    returned = returned_ref[...]
    added = dot(high_ref[...], returned) + dot(low_ref[...], returned)
    out_ref[...] = (middle_ref[...].astype(F32) + added).astype(BF16)


def shards(parts, experts, embeds, prefix_cache, w_qkv, w_up, w_down, parents, routes, gates):
    steps, rows, shard = embeds.shape
    width = w_qkv.shape[0]
    prefix = prefix_cache.shape[2]
    total = steps * rows
    used = steps * CAP
    slots = experts * used
    shape = jax.ShapeDtypeStruct

    first_expert = experts // 2 + 4
    order = [[(p + first_expert) % experts for p in range(experts)]]

    def exchange(values, axis):
        groups = order if axis == "yz" else None
        return lax.all_to_all(values, axis, split_axis=0, concat_axis=0, tiled=True, axis_index_groups=groups)

    tokens = embeds.reshape(total, shard)
    gathered = exchange(jnp.broadcast_to(tokens[None], (parts, total, shard)), "x")
    half, hidden = width // 2, w_up.shape[2]
    bias, pack, high, low, w_here, cache_here, own = call(
        functools.partial(plan_kernel, rows, steps, prefix, experts, first_expert),
        (
            shape((total, rows * prefix + HD), F32),
            shape((experts * PAD, total), BF16),
            shape((total, experts * PAD), BF16),
            shape((total, experts * PAD), BF16),
            shape((3, width, shard), BF16),
            shape(prefix_cache.shape, BF16),
            shape((half, 2 * hidden + width), BF16),
        ),
        parents,
        routes.transpose(0, 2, 1),
        gates.transpose(0, 2, 1),
        w_qkv.transpose(1, 0, 2),
        prefix_cache,
        w_up,
        w_down,
        cost=(10**8, 5 * 10**6),
        in_hbm=(3, 4, 5, 6),
        scratch=[pltpu.SemaphoreType.DMA((5,))],
    )
    other = lax.ppermute(own, "core", [(i, (i + 1) % CORES) for i in range(CORES)])
    middle, packed = call(
        functools.partial(attend_kernel, prefix),
        (shape((total, shard), BF16), shape((experts * PAD, shard), BF16)),
        gathered,
        tokens,
        w_here,
        cache_here,
        bias,
        pack,
        cost=(2 * total * width * 3 * shard, 3 * 10**6),
    )
    arrived = exchange(packed.reshape(experts, PAD, shard), "yz").reshape(experts * PAD, shard)
    spread = call(functools.partial(spread_kernel, used), shape((parts, slots, shard), BF16), arrived)
    whole = exchange(spread, "x")
    share = call(
        expert_kernel,
        shape((parts, slots, shard), BF16),
        whole,
        own,
        other,
        cost=(8 * slots * width * hidden, 6 * 10**6),
        scratch=[pltpu.VMEM((slots, width), BF16), pltpu.VMEM((slots, 2 * hidden), BF16)],
    )
    pieces = exchange(share, "x")
    summed = call(functools.partial(sum_kernel, used), shape((experts * PAD, shard), BF16), pieces)
    returned = exchange(summed.reshape(experts, PAD, shard), "yz").reshape(experts * PAD, shard)
    mixed = call(combine_kernel, shape((total, shard), BF16), middle, returned, high, low)
    return mixed.reshape(steps, rows, shard)


def solution(mesh):
    parts, devices = mesh.shape["dp"], mesh.shape["expert"]
    experts = devices // CORES
    split = Mesh(mesh.devices.reshape(parts, experts, CORES), ("x", "yz", "core"))
    rows = ("yz", "core")
    placed = (
        P(None, rows, "x"),
        P(rows, None, None, "x"),
        P(None, None, "x"),
        P(rows, None, "x"),
        P(rows, "x", None),
        P(None, rows),
        P(None, rows, None),
        P(None, rows, None),
    )
    return jax.shard_map(
        functools.partial(shards, parts, experts), mesh=split, in_specs=placed, out_specs=P(None, rows, "x"), check_vma=False
    )
```

```python
import functools

import jax
import jax.numpy as jnp
from jax import lax
from jax.experimental import pallas as pl
from jax.experimental.pallas import tpu as pltpu
from jax.sharding import Mesh
from jax.sharding import PartitionSpec as P

HD = 128
CORES = 2
BEAMS = 8
CAP = 2
PAD = 8
HIDE = -1e30
F32 = jnp.float32
BF16 = jnp.bfloat16


def iota(shape, dim):
    return lax.broadcasted_iota(jnp.int32, shape, dim)


def dot(a, b):
    return jnp.dot(a, b, preferred_element_type=F32)


def dot_last(a, b):
    return lax.dot_general(a, b, (((1,), (1,)), ((), ())), preferred_element_type=F32)


def call(kernel, outs, *args, cost=None, in_hbm=(), out_hbm=(), scratch=(), limit=16):
    flops, nbytes = cost or (0, 0)
    return pl.pallas_call(
        kernel,
        out_shape=outs,
        in_specs=[pl.BlockSpec(memory_space=pltpu.HBM if i in in_hbm else pltpu.VMEM) for i in range(len(args))],
        out_specs=[pl.BlockSpec(memory_space=pltpu.HBM if i in out_hbm else pltpu.VMEM) for i in range(len(outs))],
        scratch_shapes=scratch,
        compiler_params=pltpu.CompilerParams(vmem_limit_bytes=limit * 1024 * 1024),
        cost_estimate=pl.CostEstimate(flops=flops, bytes_accessed=nbytes, transcendentals=0),
    )(*args)


def copies_kernel(token_ref, out_ref):
    for i in range(out_ref.shape[0]):
        out_ref[i] = token_ref[...]


def plan_kernel(
    rows, steps, prefix, experts, first_expert,
    parents_ref, route_ref, gate_ref, bias_ref, pack_ref, high_ref, low_ref,
):
    total = rows * steps
    first = iota((rows, 1), 0) // BEAMS * BEAMS
    diagonal = iota((rows, rows), 0) == iota((rows, rows), 1)
    eye = diagonal.astype(F32)

    def column(row):
        return jnp.sum(jnp.where(iota((row.shape[1], row.shape[1]), 0) == iota((row.shape[1], row.shape[1]), 1), row, 0.0), axis=1, keepdims=True)

    parent = [
        (iota((rows, rows), 1) == first + column(parents_ref[t : t + 1, :].astype(F32)).astype(jnp.int32)).astype(F32).astype(BF16)
        for t in range(steps)
    ]
    none = jnp.zeros((rows, rows), F32)
    origin = []
    seen = []
    for t in range(steps):
        if t == 0:
            origin.append(parent[0].astype(F32))
            seen.append([eye] + [none] * (steps - 1))
        else:
            origin.append(dot(parent[t], origin[t - 1].astype(BF16)))
            seen.append([dot(parent[t], seen[t - 1][s].astype(BF16)) for s in range(t)] + [eye] + [none] * (steps - 1 - t))
    spread = (iota((rows, rows * prefix), 1) // prefix == iota((rows, rows * prefix), 0)).astype(F32).astype(BF16)
    old = dot(jnp.concatenate(origin, axis=0).astype(BF16), spread)
    bias_ref[:, : rows * prefix] = jnp.where(old > 0.5, 0.0, HIDE)
    new = jnp.concatenate([jnp.concatenate(seen[t], axis=1) for t in range(steps)], axis=0)
    bias_ref[:, rows * prefix :] = jnp.full((total, HD), HIDE, F32)
    bias_ref[:, rows * prefix : rows * prefix + total] = jnp.where(new > 0.5, 0.0, HIDE)

    a, b = iota((total, total), 0), iota((total, total), 1)
    same = a // rows == b // rows
    after = (same & (a < b)).astype(F32).astype(BF16)
    places = [
        jnp.concatenate([(route_ref[t, k : k + 1, :] + (experts - first_expert)) % experts for t in range(steps)], axis=1)
        for k in range(2)
    ]
    gates = [jnp.concatenate([gate_ref[t, k : k + 1, :] for t in range(steps)], axis=1) for k in range(2)]
    named = [(iota((experts, total), 0) == places[k]).astype(F32) for k in range(2)]
    count = dot((named[0] + named[1]).astype(BF16), after)
    step_at = (iota((1, total), 1) // rows) * CAP
    chosen = jnp.zeros((experts * PAD, total), F32)
    weights = jnp.zeros((total, experts * PAD), F32)
    for k in range(2):
        order = jnp.sum(named[k] * count, axis=0, keepdims=True).astype(jnp.int32)
        target = places[k] * PAD + step_at + order
        chosen += (iota((experts * PAD, total), 0) == target).astype(F32)
        at = column(target.astype(F32)).astype(jnp.int32)
        weights += jnp.where(iota((total, experts * PAD), 1) == at, column(gates[k]), 0.0)
    pack_ref[...] = chosen.astype(BF16)
    high = weights.astype(BF16)
    high_ref[...] = high
    low_ref[...] = (weights - high.astype(F32)).astype(BF16)


def normed_blocks(blocks):
    width = sum(v.shape[-1] for v in blocks)
    mean = sum(jnp.sum(v, axis=-1, keepdims=True) for v in blocks) / width
    centred = [v - mean for v in blocks]
    spread = sum(jnp.sum(v * v, axis=-1, keepdims=True) for v in centred) / width
    scale = lax.rsqrt(spread + 1e-05)
    return jnp.concatenate([(v * scale).astype(BF16) for v in centred], axis=-1)


def attend_kernel(prefix, gathered_ref, token_ref, w_ref, cache_ref, bias_ref, pack_ref, middle_ref, packed_ref):
    parts = gathered_ref.shape[0]
    total, shard = token_ref.shape
    rows = cache_ref.shape[0]
    normed = normed_blocks([gathered_ref[i].astype(F32) for i in range(parts)])
    query, key, value = (dot(normed, w_ref[j]).astype(BF16) for j in range(3))
    bias_old = bias_ref[:, : rows * prefix]
    bias_new = bias_ref[:, rows * prefix : rows * prefix + total]
    for h in range(shard // HD):
        at = slice(h * HD, (h + 1) * HD)
        old_keys = cache_ref[:, 0, :, at].reshape(rows * prefix, HD)
        old_values = cache_ref[:, 1, :, at].reshape(rows * prefix, HD)
        w_old = jnp.exp(dot_last(query[:, at], old_keys) * HD ** (-0.5) + bias_old)
        w_new = jnp.exp(dot_last(query[:, at], key[:, at]) * HD ** (-0.5) + bias_new)
        weight = jnp.sum(w_old, axis=-1, keepdims=True) + jnp.sum(w_new, axis=-1, keepdims=True)
        summed = dot(w_old.astype(BF16), old_values) + dot(w_new.astype(BF16), value[:, at])
        middle_ref[:, at] = (token_ref[:, at].astype(F32) + summed / weight).astype(BF16)
    packed_ref[...] = dot(pack_ref[...], middle_ref[...]).astype(BF16)


def spread_kernel(used, arrived_ref, out_ref):
    group = 8
    keep = (iota((group * used, group * PAD), 1) == (iota((group * used, 1), 0) // used) * PAD + iota((group * used, 1), 0) % used)
    keep = keep.astype(F32).astype(BF16)
    for g in range(arrived_ref.shape[0] // (group * PAD)):
        block = dot(keep, arrived_ref[g * group * PAD : (g + 1) * group * PAD, :]).astype(BF16)
        for i in range(out_ref.shape[0]):
            out_ref[i, g * group * used : (g + 1) * group * used, :] = block


def expert_kernel(
    slots_ref, up_ref, down_ref, up_other_hbm, down_other_hbm,
    out_ref, normed_ref, hidden_ref, sum_ref, up_other_ref, down_other_ref, sems,
):
    parts, slots, shard = slots_ref.shape
    width, units = up_ref.shape[1:]
    copies = []
    for source, target in ((up_other_hbm, up_other_ref), (down_other_hbm, down_other_ref)):
        rows = source.shape[1] // 4
        for g in range(4):
            at = (0, slice(g * rows, (g + 1) * rows))
            copies.append(pltpu.make_async_copy(source.at[at], target.at[at], sems.at[len(copies)]))
    for copy in copies:
        copy.start()
    block = slots // 3
    for g in range(slots // block):
        at = slice(g * block, (g + 1) * block)
        normed_ref[at, :] = normed_blocks([slots_ref[i, at, :].astype(F32) for i in range(parts)])
    wide = 256

    def hide(ref):
        for n in range(0, units, wide):
            hidden_ref[:, n : n + wide] = jax.nn.relu(dot(normed_ref[...], ref[0, :, n : n + wide])).astype(BF16)

    hide(up_ref)
    for i in range(parts):
        at = slice(i * shard, (i + 1) * shard)
        sum_ref[:, at] = dot(hidden_ref[...], down_ref[0, :, at])
    for copy in copies[:4]:
        copy.wait()
    hide(up_other_ref)
    for copy in copies[4:]:
        copy.wait()
    for i in range(parts):
        at = slice(i * shard, (i + 1) * shard)
        out_ref[i] = (sum_ref[:, at] + dot(hidden_ref[...], down_other_ref[0, :, at])).astype(BF16)


def sum_kernel(used, parts_ref, out_ref):
    group = 8
    place = (iota((group * PAD, group * used), 0) == (iota((1, group * used), 1) // used) * PAD + iota((1, group * used), 1) % used)
    place = place.astype(F32).astype(BF16)
    for g in range(out_ref.shape[0] // (group * PAD)):
        at = slice(g * group * used, (g + 1) * group * used)
        total = sum(parts_ref[i, at, :].astype(F32) for i in range(parts_ref.shape[0]))
        out_ref[g * group * PAD : (g + 1) * group * PAD, :] = dot(place, total.astype(BF16)).astype(BF16)


def combine_kernel(middle_ref, returned_ref, high_ref, low_ref, out_ref):
    returned = returned_ref[...]
    added = dot(high_ref[...], returned) + dot(low_ref[...], returned)
    out_ref[...] = (middle_ref[...].astype(F32) + added).astype(BF16)


def shards(parts, experts, embeds, prefix_cache, w_qkv, w_up, w_down, parents, routes, gates):
    steps, rows, shard = embeds.shape
    width = w_qkv.shape[0]
    prefix = prefix_cache.shape[2]
    total = steps * rows
    used = steps * CAP
    slots = experts * used
    shape = jax.ShapeDtypeStruct

    first_expert = experts // 2 + 4
    order = [[(p + first_expert) % experts for p in range(experts)]]

    def exchange(values, axis):
        groups = order if axis == "yz" else None
        return lax.all_to_all(values, axis, split_axis=0, concat_axis=0, tiled=True, axis_index_groups=groups)

    tokens = embeds.reshape(total, shard)
    (copies,) = call(copies_kernel, [shape((parts, total, shard), BF16)], tokens, cost=(10**9, 10**7))
    gathered = exchange(copies, "x")
    hidden = w_up.shape[2]
    swap = [(i, (i + 1) % CORES) for i in range(CORES)]
    up_other = lax.ppermute(w_up, "core", swap)
    down_other = lax.ppermute(w_down, "core", swap)
    bias, pack, high, low = call(
        functools.partial(plan_kernel, rows, steps, prefix, experts, first_expert),
        (
            shape((total, rows * prefix + HD), F32),
            shape((experts * PAD, total), BF16),
            shape((total, experts * PAD), BF16),
            shape((total, experts * PAD), BF16),
        ),
        parents,
        routes.transpose(0, 2, 1),
        gates.transpose(0, 2, 1),
        cost=(10**9, 10**7),
    )
    gathered, up_other, down_other = lax.optimization_barrier((gathered, up_other, down_other))
    middle, packed = call(
        functools.partial(attend_kernel, prefix),
        (shape((total, shard), BF16), shape((experts * PAD, shard), BF16)),
        gathered,
        tokens,
        w_qkv.transpose(1, 0, 2),
        prefix_cache,
        bias,
        pack,
        cost=(2 * total * width * 3 * shard, 3 * 10**6),
    )
    arrived = exchange(packed.reshape(experts, PAD, shard), "yz").reshape(experts * PAD, shard)
    (spread,) = call(functools.partial(spread_kernel, used), [shape((parts, slots, shard), BF16)], arrived)
    whole = exchange(spread, "x")
    (share,) = call(
        expert_kernel,
        [shape((parts, slots, shard), BF16)],
        whole,
        w_up,
        w_down,
        up_other,
        down_other,
        cost=(8 * slots * width * hidden, 6 * 10**6),
        in_hbm=(3, 4),
        scratch=[
            pltpu.VMEM((slots, width), BF16),
            pltpu.VMEM((slots, hidden), BF16),
            pltpu.VMEM((slots, width), F32),
            pltpu.VMEM(w_up.shape, BF16),
            pltpu.VMEM(w_down.shape, BF16),
            pltpu.SemaphoreType.DMA((8,)),
        ],
    )
    pieces = exchange(share, "x")
    (summed,) = call(functools.partial(sum_kernel, used), [shape((experts * PAD, shard), BF16)], pieces)
    returned = exchange(summed.reshape(experts, PAD, shard), "yz").reshape(experts * PAD, shard)
    (mixed,) = call(combine_kernel, [shape((total, shard), BF16)], middle, returned, high, low)
    return mixed.reshape(steps, rows, shard)


def solution(mesh):
    parts, devices = mesh.shape["dp"], mesh.shape["expert"]
    experts = devices // CORES
    split = Mesh(mesh.devices.reshape(parts, experts, CORES), ("x", "yz", "core"))
    rows = ("yz", "core")
    placed = (
        P(None, rows, "x"),
        P(rows, None, None, "x"),
        P(None, None, "x"),
        P(rows, None, "x"),
        P(rows, "x", None),
        P(None, rows),
        P(None, rows, None),
        P(None, rows, None),
    )
    return jax.shard_map(
        functools.partial(shards, parts, experts), mesh=split, in_specs=placed, out_specs=P(None, rows, "x"), check_vma=False
    )
```

```python
import functools

import jax
import jax.numpy as jnp
from jax import lax
from jax.experimental import pallas as pl
from jax.experimental.pallas import tpu as pltpu
from jax.sharding import Mesh
from jax.sharding import PartitionSpec as P

HD = 128
CORES = 2
BEAMS = 8
CAP = 2
PAD = 8
HIDE = -1e30
F32 = jnp.float32
BF16 = jnp.bfloat16


def iota(shape, dim):
    return lax.broadcasted_iota(jnp.int32, shape, dim)


def dot(a, b):
    return jnp.dot(a, b, preferred_element_type=F32)


def dot_last(a, b):
    return lax.dot_general(a, b, (((1,), (1,)), ((), ())), preferred_element_type=F32)


def call(kernel, outs, *args, cost=None, in_hbm=(), out_hbm=(), scratch=(), limit=16):
    flops, nbytes = cost or (0, 0)
    return pl.pallas_call(
        kernel,
        out_shape=outs,
        in_specs=[pl.BlockSpec(memory_space=pltpu.HBM if i in in_hbm else pltpu.VMEM) for i in range(len(args))],
        out_specs=[pl.BlockSpec(memory_space=pltpu.HBM if i in out_hbm else pltpu.VMEM) for i in range(len(outs))],
        scratch_shapes=scratch,
        compiler_params=pltpu.CompilerParams(vmem_limit_bytes=limit * 1024 * 1024),
        cost_estimate=pl.CostEstimate(flops=flops, bytes_accessed=nbytes, transcendentals=0),
    )(*args)


def copies_kernel(token_ref, out_ref):
    for i in range(out_ref.shape[0]):
        out_ref[i] = token_ref[...]


def plan_kernel(
    rows, steps, prefix, experts, first_expert,
    parents_ref, route_ref, gate_ref, bias_ref, pack_ref, high_ref, low_ref,
):
    total = rows * steps
    first = iota((rows, 1), 0) // BEAMS * BEAMS
    diagonal = iota((rows, rows), 0) == iota((rows, rows), 1)
    eye = diagonal.astype(F32)

    def column(row):
        return jnp.sum(jnp.where(iota((row.shape[1], row.shape[1]), 0) == iota((row.shape[1], row.shape[1]), 1), row, 0.0), axis=1, keepdims=True)

    parent = [
        (iota((rows, rows), 1) == first + column(parents_ref[t : t + 1, :].astype(F32)).astype(jnp.int32)).astype(F32).astype(BF16)
        for t in range(steps)
    ]
    none = jnp.zeros((rows, rows), F32)
    origin = []
    seen = []
    for t in range(steps):
        if t == 0:
            origin.append(parent[0].astype(F32))
            seen.append([eye] + [none] * (steps - 1))
        else:
            origin.append(dot(parent[t], origin[t - 1].astype(BF16)))
            seen.append([dot(parent[t], seen[t - 1][s].astype(BF16)) for s in range(t)] + [eye] + [none] * (steps - 1 - t))
    spread = (iota((rows, rows * prefix), 1) // prefix == iota((rows, rows * prefix), 0)).astype(F32).astype(BF16)
    old = dot(jnp.concatenate(origin, axis=0).astype(BF16), spread)
    bias_ref[:, : rows * prefix] = jnp.where(old > 0.5, 0.0, HIDE)
    new = jnp.concatenate([jnp.concatenate(seen[t], axis=1) for t in range(steps)], axis=0)
    bias_ref[:, rows * prefix :] = jnp.full((total, HD), HIDE, F32)
    bias_ref[:, rows * prefix : rows * prefix + total] = jnp.where(new > 0.5, 0.0, HIDE)

    a, b = iota((total, total), 0), iota((total, total), 1)
    same = a // rows == b // rows
    after = (same & (a < b)).astype(F32).astype(BF16)
    places = [
        jnp.concatenate([(route_ref[t, k : k + 1, :] + (experts - first_expert)) % experts for t in range(steps)], axis=1)
        for k in range(2)
    ]
    gates = [jnp.concatenate([gate_ref[t, k : k + 1, :] for t in range(steps)], axis=1) for k in range(2)]
    named = [(iota((experts, total), 0) == places[k]).astype(F32) for k in range(2)]
    count = dot((named[0] + named[1]).astype(BF16), after)
    step_at = (iota((1, total), 1) // rows) * CAP
    chosen = jnp.zeros((experts * PAD, total), F32)
    weights = jnp.zeros((total, experts * PAD), F32)
    for k in range(2):
        order = jnp.sum(named[k] * count, axis=0, keepdims=True).astype(jnp.int32)
        target = places[k] * PAD + step_at + order
        chosen += (iota((experts * PAD, total), 0) == target).astype(F32)
        at = column(target.astype(F32)).astype(jnp.int32)
        weights += jnp.where(iota((total, experts * PAD), 1) == at, column(gates[k]), 0.0)
    pack_ref[...] = chosen.astype(BF16)
    high = weights.astype(BF16)
    high_ref[...] = high
    low_ref[...] = (weights - high.astype(F32)).astype(BF16)


def normed_blocks(blocks):
    width = sum(v.shape[-1] for v in blocks)
    mean = sum(jnp.sum(v, axis=-1, keepdims=True) for v in blocks) / width
    centred = [v - mean for v in blocks]
    spread = sum(jnp.sum(v * v, axis=-1, keepdims=True) for v in centred) / width
    scale = lax.rsqrt(spread + 1e-05)
    return jnp.concatenate([(v * scale).astype(BF16) for v in centred], axis=-1)


def attend_kernel(prefix, gathered_ref, token_ref, w_ref, cache_ref, bias_ref, pack_ref, middle_ref, packed_ref):
    parts = gathered_ref.shape[0]
    total, shard = token_ref.shape
    rows = cache_ref.shape[0]
    normed = normed_blocks([gathered_ref[i].astype(F32) for i in range(parts)])
    query, key, value = (dot(normed, w_ref[j]).astype(BF16) for j in range(3))
    bias_old = bias_ref[:, : rows * prefix]
    bias_new = bias_ref[:, rows * prefix : rows * prefix + total]
    for h in range(shard // HD):
        at = slice(h * HD, (h + 1) * HD)
        old_keys = cache_ref[:, 0, :, at].reshape(rows * prefix, HD)
        old_values = cache_ref[:, 1, :, at].reshape(rows * prefix, HD)
        w_old = jnp.exp(dot_last(query[:, at], old_keys) * HD ** (-0.5) + bias_old)
        w_new = jnp.exp(dot_last(query[:, at], key[:, at]) * HD ** (-0.5) + bias_new)
        weight = jnp.sum(w_old, axis=-1, keepdims=True) + jnp.sum(w_new, axis=-1, keepdims=True)
        summed = dot(w_old.astype(BF16), old_values) + dot(w_new.astype(BF16), value[:, at])
        middle_ref[:, at] = (token_ref[:, at].astype(F32) + summed / weight).astype(BF16)
    packed_ref[...] = dot(pack_ref[...], middle_ref[...]).astype(BF16)


def spread_kernel(used, arrived_ref, out_ref):
    group = 8
    keep = (iota((group * used, group * PAD), 1) == (iota((group * used, 1), 0) // used) * PAD + iota((group * used, 1), 0) % used)
    keep = keep.astype(F32).astype(BF16)
    for g in range(arrived_ref.shape[0] // (group * PAD)):
        block = dot(keep, arrived_ref[g * group * PAD : (g + 1) * group * PAD, :]).astype(BF16)
        for i in range(out_ref.shape[0]):
            out_ref[i, g * group * used : (g + 1) * group * used, :] = block


def norm_kernel(slots_ref, up_hbm, normed_ref, up_ref, sem):
    copy = pltpu.make_async_copy(up_hbm, up_ref, sem)
    copy.start()
    parts, slots, _ = slots_ref.shape
    block = slots // 3
    for g in range(slots // block):
        at = slice(g * block, (g + 1) * block)
        normed_ref[at, :] = normed_blocks([slots_ref[i, at, :].astype(F32) for i in range(parts)])
    copy.wait()


def own_half_kernel(normed_ref, up_ref, down_ref, sum_ref, hidden_ref):
    units, width = down_ref.shape[1:]
    wide = 256
    for n in range(0, units, wide):
        at = slice(n, n + wide)
        hidden_ref[:, at] = jax.nn.relu(dot(normed_ref[...], up_ref[0, :, at])).astype(BF16)
    for n in range(0, width, wide):
        at = slice(n, n + wide)
        sum_ref[:, at] = dot(hidden_ref[...], down_ref[0, :, at])


def other_half_kernel(normed_ref, sum_ref, up_ref, down_ref, out_ref, hidden_ref):
    units, width = down_ref.shape[1:]
    wide = width // out_ref.shape[0]
    for n in range(0, units, wide):
        at = slice(n, n + wide)
        hidden_ref[:, at] = jax.nn.relu(dot(normed_ref[...], up_ref[0, :, at])).astype(BF16)
    for i in range(out_ref.shape[0]):
        at = slice(i * wide, (i + 1) * wide)
        out_ref[i] = (sum_ref[:, at] + dot(hidden_ref[...], down_ref[0, :, at])).astype(BF16)


def sum_kernel(used, parts_ref, out_ref):
    group = 8
    place = (iota((group * PAD, group * used), 0) == (iota((1, group * used), 1) // used) * PAD + iota((1, group * used), 1) % used)
    place = place.astype(F32).astype(BF16)
    for g in range(out_ref.shape[0] // (group * PAD)):
        at = slice(g * group * used, (g + 1) * group * used)
        total = sum(parts_ref[i, at, :].astype(F32) for i in range(parts_ref.shape[0]))
        out_ref[g * group * PAD : (g + 1) * group * PAD, :] = dot(place, total.astype(BF16)).astype(BF16)


def combine_kernel(middle_ref, returned_ref, high_ref, low_ref, out_ref):
    returned = returned_ref[...]
    added = dot(high_ref[...], returned) + dot(low_ref[...], returned)
    out_ref[...] = (middle_ref[...].astype(F32) + added).astype(BF16)


def shards(parts, experts, embeds, prefix_cache, w_qkv, w_up, w_down, parents, routes, gates):
    steps, rows, shard = embeds.shape
    width = w_qkv.shape[0]
    prefix = prefix_cache.shape[2]
    total = steps * rows
    used = steps * CAP
    slots = experts * used
    shape = jax.ShapeDtypeStruct

    first_expert = experts // 2 + 4
    order = [[(p + first_expert) % experts for p in range(experts)]]

    def exchange(values, axis):
        groups = order if axis == "yz" else None
        return lax.all_to_all(values, axis, split_axis=0, concat_axis=0, tiled=True, axis_index_groups=groups)

    tokens = embeds.reshape(total, shard)
    (copies,) = call(copies_kernel, [shape((parts, total, shard), BF16)], tokens, cost=(10**9, 10**7))
    gathered = exchange(copies, "x")
    hidden = w_up.shape[2]
    swap = [(i, (i + 1) % CORES) for i in range(CORES)]
    up_other = lax.ppermute(w_up, "core", swap)
    down_other = lax.ppermute(w_down, "core", swap)
    bias, pack, high, low = call(
        functools.partial(plan_kernel, rows, steps, prefix, experts, first_expert),
        (
            shape((total, rows * prefix + HD), F32),
            shape((experts * PAD, total), BF16),
            shape((total, experts * PAD), BF16),
            shape((total, experts * PAD), BF16),
        ),
        parents,
        routes.transpose(0, 2, 1),
        gates.transpose(0, 2, 1),
        cost=(10**9, 10**7),
    )
    middle, packed = call(
        functools.partial(attend_kernel, prefix),
        (shape((total, shard), BF16), shape((experts * PAD, shard), BF16)),
        gathered,
        tokens,
        w_qkv.transpose(1, 0, 2),
        prefix_cache,
        bias,
        pack,
        cost=(2 * total * width * 3 * shard, 3 * 10**6),
    )
    arrived = exchange(packed.reshape(experts, PAD, shard), "yz").reshape(experts * PAD, shard)
    (spread,) = call(functools.partial(spread_kernel, used), [shape((parts, slots, shard), BF16)], arrived)
    whole = exchange(spread, "x")
    normed, up_own = call(
        norm_kernel,
        [shape((slots, width), BF16), shape(w_up.shape, BF16)],
        whole,
        w_up,
        cost=(10**9, 10**7),
        in_hbm=(1,),
        scratch=[pltpu.SemaphoreType.DMA],
    )
    (half,) = call(
        own_half_kernel,
        [shape((slots, width), F32)],
        normed,
        up_own,
        w_down,
        cost=(10**11, 10**7),
        scratch=[pltpu.VMEM((slots, hidden), BF16)],
    )
    (share,) = call(
        other_half_kernel,
        [shape((parts, slots, shard), BF16)],
        normed,
        half,
        up_other,
        down_other,
        cost=(4 * slots * width * hidden, 6 * 10**6),
        scratch=[pltpu.VMEM((slots, hidden), BF16)],
    )
    pieces = exchange(share, "x")
    (summed,) = call(functools.partial(sum_kernel, used), [shape((experts * PAD, shard), BF16)], pieces)
    returned = exchange(summed.reshape(experts, PAD, shard), "yz").reshape(experts * PAD, shard)
    (mixed,) = call(combine_kernel, [shape((total, shard), BF16)], middle, returned, high, low)
    return mixed.reshape(steps, rows, shard)


def solution(mesh):
    parts, devices = mesh.shape["dp"], mesh.shape["expert"]
    experts = devices // CORES
    split = Mesh(mesh.devices.reshape(parts, experts, CORES), ("x", "yz", "core"))
    rows = ("yz", "core")
    placed = (
        P(None, rows, "x"),
        P(rows, None, None, "x"),
        P(None, None, "x"),
        P(rows, None, "x"),
        P(rows, "x", None),
        P(None, rows),
        P(None, rows, None),
        P(None, rows, None),
    )
    return jax.shard_map(
        functools.partial(shards, parts, experts), mesh=split, in_specs=placed, out_specs=P(None, rows, "x"), check_vma=False
    )
```

```python
import functools

import jax
import jax.numpy as jnp
from jax import lax
from jax.experimental import pallas as pl
from jax.experimental.pallas import tpu as pltpu
from jax.sharding import Mesh
from jax.sharding import PartitionSpec as P

HD = 128
CORES = 2
BEAMS = 8
CAP = 2
PAD = 8
HIDE = -1e30
F32 = jnp.float32
BF16 = jnp.bfloat16


def iota(shape, dim):
    return lax.broadcasted_iota(jnp.int32, shape, dim)


def dot(a, b):
    return jnp.dot(a, b, preferred_element_type=F32)


def dot_last(a, b):
    return lax.dot_general(a, b, (((1,), (1,)), ((), ())), preferred_element_type=F32)


def call(kernel, outs, *args, cost=None, in_hbm=(), out_hbm=(), scratch=(), limit=16):
    flops, nbytes = cost or (0, 0)
    return pl.pallas_call(
        kernel,
        out_shape=outs,
        in_specs=[pl.BlockSpec(memory_space=pltpu.HBM if i in in_hbm else pltpu.VMEM) for i in range(len(args))],
        out_specs=[pl.BlockSpec(memory_space=pltpu.HBM if i in out_hbm else pltpu.VMEM) for i in range(len(outs))],
        scratch_shapes=scratch,
        compiler_params=pltpu.CompilerParams(vmem_limit_bytes=limit * 1024 * 1024),
        cost_estimate=pl.CostEstimate(flops=flops, bytes_accessed=nbytes, transcendentals=0),
    )(*args)


def place_of(device, parts):
    return (device + parts // 2) % parts


def copies_kernel(token_ref, out_ref):
    for i in range(out_ref.shape[0]):
        out_ref[i] = token_ref[...]


def plan_kernel(
    rows, steps, prefix, experts, first_expert,
    parents_ref, route_ref, gate_ref, bias_ref, pack_ref, high_ref, low_ref,
):
    total = rows * steps
    first = iota((rows, 1), 0) // BEAMS * BEAMS
    diagonal = iota((rows, rows), 0) == iota((rows, rows), 1)
    eye = diagonal.astype(F32)

    def column(row):
        return jnp.sum(jnp.where(iota((row.shape[1], row.shape[1]), 0) == iota((row.shape[1], row.shape[1]), 1), row, 0.0), axis=1, keepdims=True)

    parent = [
        (iota((rows, rows), 1) == first + column(parents_ref[t : t + 1, :].astype(F32)).astype(jnp.int32)).astype(F32).astype(BF16)
        for t in range(steps)
    ]
    none = jnp.zeros((rows, rows), F32)
    origin = []
    seen = []
    for t in range(steps):
        if t == 0:
            origin.append(parent[0].astype(F32))
            seen.append([eye] + [none] * (steps - 1))
        else:
            origin.append(dot(parent[t], origin[t - 1].astype(BF16)))
            seen.append([dot(parent[t], seen[t - 1][s].astype(BF16)) for s in range(t)] + [eye] + [none] * (steps - 1 - t))
    spread = (iota((rows, rows * prefix), 1) // prefix == iota((rows, rows * prefix), 0)).astype(F32).astype(BF16)
    old = dot(jnp.concatenate(origin, axis=0).astype(BF16), spread)
    bias_ref[:, : rows * prefix] = jnp.where(old > 0.5, 0.0, HIDE)
    new = jnp.concatenate([jnp.concatenate(seen[t], axis=1) for t in range(steps)], axis=0)
    bias_ref[:, rows * prefix :] = jnp.full((total, HD), HIDE, F32)
    bias_ref[:, rows * prefix : rows * prefix + total] = jnp.where(new > 0.5, 0.0, HIDE)

    a, b = iota((total, total), 0), iota((total, total), 1)
    same = a // rows == b // rows
    after = (same & (a < b)).astype(F32).astype(BF16)
    places = [
        jnp.concatenate([(route_ref[t, k : k + 1, :] + (experts - first_expert)) % experts for t in range(steps)], axis=1)
        for k in range(2)
    ]
    gates = [jnp.concatenate([gate_ref[t, k : k + 1, :] for t in range(steps)], axis=1) for k in range(2)]
    named = [(iota((experts, total), 0) == places[k]).astype(F32) for k in range(2)]
    count = dot((named[0] + named[1]).astype(BF16), after)
    step_at = (iota((1, total), 1) // rows) * CAP
    chosen = jnp.zeros((experts * PAD, total), F32)
    weights = jnp.zeros((total, experts * PAD), F32)
    for k in range(2):
        order = jnp.sum(named[k] * count, axis=0, keepdims=True).astype(jnp.int32)
        target = places[k] * PAD + step_at + order
        chosen += (iota((experts * PAD, total), 0) == target).astype(F32)
        at = column(target.astype(F32)).astype(jnp.int32)
        weights += jnp.where(iota((total, experts * PAD), 1) == at, column(gates[k]), 0.0)
    pack_ref[...] = chosen.astype(BF16)
    high = weights.astype(BF16)
    high_ref[...] = high
    low_ref[...] = (weights - high.astype(F32)).astype(BF16)


def normed_blocks(blocks):
    width = sum(v.shape[-1] for v in blocks)
    mean = sum(jnp.sum(v, axis=-1, keepdims=True) for v in blocks) / width
    centred = [v - mean for v in blocks]
    spread = sum(jnp.sum(v * v, axis=-1, keepdims=True) for v in centred) / width
    scale = lax.rsqrt(spread + 1e-05)
    return jnp.concatenate([(v * scale).astype(BF16) for v in centred], axis=-1)


def attend_kernel(prefix, gathered_ref, token_ref, w_ref, cache_ref, bias_ref, pack_ref, middle_ref, packed_ref):
    parts = gathered_ref.shape[0]
    total, shard = token_ref.shape
    rows = cache_ref.shape[0]
    normed = normed_blocks([gathered_ref[place_of(i, parts)].astype(F32) for i in range(parts)])
    query, key, value = (dot(normed, w_ref[j]).astype(BF16) for j in range(3))
    bias_old = bias_ref[:, : rows * prefix]
    bias_new = bias_ref[:, rows * prefix : rows * prefix + total]
    for h in range(shard // HD):
        at = slice(h * HD, (h + 1) * HD)
        old_keys = cache_ref[:, 0, :, at].reshape(rows * prefix, HD)
        old_values = cache_ref[:, 1, :, at].reshape(rows * prefix, HD)
        w_old = jnp.exp(dot_last(query[:, at], old_keys) * HD ** (-0.5) + bias_old)
        w_new = jnp.exp(dot_last(query[:, at], key[:, at]) * HD ** (-0.5) + bias_new)
        weight = jnp.sum(w_old, axis=-1, keepdims=True) + jnp.sum(w_new, axis=-1, keepdims=True)
        summed = dot(w_old.astype(BF16), old_values) + dot(w_new.astype(BF16), value[:, at])
        middle_ref[:, at] = (token_ref[:, at].astype(F32) + summed / weight).astype(BF16)
    packed_ref[...] = dot(pack_ref[...], middle_ref[...]).astype(BF16)


def spread_kernel(used, arrived_ref, out_ref):
    group = 8
    keep = (iota((group * used, group * PAD), 1) == (iota((group * used, 1), 0) // used) * PAD + iota((group * used, 1), 0) % used)
    keep = keep.astype(F32).astype(BF16)
    for g in range(arrived_ref.shape[0] // (group * PAD)):
        block = dot(keep, arrived_ref[g * group * PAD : (g + 1) * group * PAD, :]).astype(BF16)
        for i in range(out_ref.shape[0]):
            out_ref[i, g * group * used : (g + 1) * group * used, :] = block


def norm_kernel(slots_ref, up_hbm, normed_ref, up_ref, sem):
    copy = pltpu.make_async_copy(up_hbm, up_ref, sem)
    copy.start()
    parts, slots, _ = slots_ref.shape
    block = slots // 3
    for g in range(slots // block):
        at = slice(g * block, (g + 1) * block)
        normed_ref[at, :] = normed_blocks([slots_ref[place_of(i, parts), at, :].astype(F32) for i in range(parts)])
    copy.wait()


def own_half_kernel(normed_ref, up_ref, down_ref, sum_ref, hidden_ref):
    units, width = down_ref.shape[1:]
    wide = 256
    for n in range(0, units, wide):
        at = slice(n, n + wide)
        hidden_ref[:, at] = jax.nn.relu(dot(normed_ref[...], up_ref[0, :, at])).astype(BF16)
    for n in range(0, width, wide):
        at = slice(n, n + wide)
        sum_ref[:, at] = dot(hidden_ref[...], down_ref[0, :, at])


def other_half_kernel(normed_ref, sum_ref, up_ref, down_ref, out_ref, hidden_ref):
    units, width = down_ref.shape[1:]
    wide = width // out_ref.shape[0]
    for n in range(0, units, wide):
        at = slice(n, n + wide)
        hidden_ref[:, at] = jax.nn.relu(dot(normed_ref[...], up_ref[0, :, at])).astype(BF16)
    for i in range(out_ref.shape[0]):
        at = slice(i * wide, (i + 1) * wide)
        out_ref[place_of(i, out_ref.shape[0])] = (sum_ref[:, at] + dot(hidden_ref[...], down_ref[0, :, at])).astype(BF16)


def sum_kernel(used, parts_ref, out_ref):
    group = 8
    place = (iota((group * PAD, group * used), 0) == (iota((1, group * used), 1) // used) * PAD + iota((1, group * used), 1) % used)
    place = place.astype(F32).astype(BF16)
    for g in range(out_ref.shape[0] // (group * PAD)):
        at = slice(g * group * used, (g + 1) * group * used)
        total = sum(parts_ref[i, at, :].astype(F32) for i in range(parts_ref.shape[0]))
        out_ref[g * group * PAD : (g + 1) * group * PAD, :] = dot(place, total.astype(BF16)).astype(BF16)


def combine_kernel(middle_ref, returned_ref, high_ref, low_ref, out_ref):
    total = middle_ref.shape[0]
    both = dot(jnp.concatenate([high_ref[...], low_ref[...]], axis=0), returned_ref[...])
    added = both[:total] + both[total:]
    out_ref[...] = (middle_ref[...].astype(F32) + added).astype(BF16)


def shards(parts, experts, embeds, prefix_cache, w_qkv, w_up, w_down, parents, routes, gates):
    steps, rows, shard = embeds.shape
    width = w_qkv.shape[0]
    prefix = prefix_cache.shape[2]
    total = steps * rows
    used = steps * CAP
    slots = experts * used
    shape = jax.ShapeDtypeStruct

    first_expert = experts // 2 + 4
    order = [[(p + first_expert) % experts for p in range(experts)]]

    def exchange(values, axis):
        groups = order if axis == "yz" else [[place_of(p, parts) for p in range(parts)]]
        return lax.all_to_all(values, axis, split_axis=0, concat_axis=0, tiled=True, axis_index_groups=groups)

    tokens = embeds.reshape(total, shard)
    (copies,) = call(copies_kernel, [shape((parts, total, shard), BF16)], tokens, cost=(10**9, 10**7))
    gathered = exchange(copies, "x")
    hidden = w_up.shape[2]
    swap = [(i, (i + 1) % CORES) for i in range(CORES)]
    up_other = lax.ppermute(w_up, "core", swap)
    down_other = lax.ppermute(w_down, "core", swap)
    bias, pack, high, low = call(
        functools.partial(plan_kernel, rows, steps, prefix, experts, first_expert),
        (
            shape((total, rows * prefix + HD), F32),
            shape((experts * PAD, total), BF16),
            shape((total, experts * PAD), BF16),
            shape((total, experts * PAD), BF16),
        ),
        parents,
        routes.transpose(0, 2, 1),
        gates.transpose(0, 2, 1),
        cost=(10**9, 10**7),
    )
    middle, packed = call(
        functools.partial(attend_kernel, prefix),
        (shape((total, shard), BF16), shape((experts * PAD, shard), BF16)),
        gathered,
        tokens,
        w_qkv.transpose(1, 0, 2),
        prefix_cache,
        bias,
        pack,
        cost=(2 * total * width * 3 * shard, 3 * 10**6),
    )
    arrived = exchange(packed.reshape(experts, PAD, shard), "yz").reshape(experts * PAD, shard)
    (spread,) = call(functools.partial(spread_kernel, used), [shape((parts, slots, shard), BF16)], arrived)
    whole = exchange(spread, "x")
    normed, up_own = call(
        norm_kernel,
        [shape((slots, width), BF16), shape(w_up.shape, BF16)],
        whole,
        w_up,
        cost=(10**9, 10**7),
        in_hbm=(1,),
        scratch=[pltpu.SemaphoreType.DMA],
    )
    (half,) = call(
        own_half_kernel,
        [shape((slots, width), F32)],
        normed,
        up_own,
        w_down,
        cost=(10**11, 10**7),
        scratch=[pltpu.VMEM((slots, hidden), BF16)],
    )
    (share,) = call(
        other_half_kernel,
        [shape((parts, slots, shard), BF16)],
        normed,
        half,
        up_other,
        down_other,
        cost=(4 * slots * width * hidden, 6 * 10**6),
        scratch=[pltpu.VMEM((slots, hidden), BF16)],
    )
    pieces = exchange(share, "x")
    (summed,) = call(functools.partial(sum_kernel, used), [shape((experts * PAD, shard), BF16)], pieces)
    returned = exchange(summed.reshape(experts, PAD, shard), "yz").reshape(experts * PAD, shard)
    (mixed,) = call(combine_kernel, [shape((total, shard), BF16)], middle, returned, high, low)
    return mixed.reshape(steps, rows, shard)


def solution(mesh):
    parts, devices = mesh.shape["dp"], mesh.shape["expert"]
    experts = devices // CORES
    split = Mesh(mesh.devices.reshape(parts, experts, CORES), ("x", "yz", "core"))
    rows = ("yz", "core")
    placed = (
        P(None, rows, "x"),
        P(rows, None, None, "x"),
        P(None, None, "x"),
        P(rows, None, "x"),
        P(rows, "x", None),
        P(None, rows),
        P(None, rows, None),
        P(None, rows, None),
    )
    return jax.shard_map(
        functools.partial(shards, parts, experts), mesh=split, in_specs=placed, out_specs=P(None, rows, "x"), check_vma=False
    )
```

```python
import functools

import jax
import jax.numpy as jnp
from jax import lax
from jax.experimental import pallas as pl
from jax.experimental.pallas import tpu as pltpu
from jax.sharding import Mesh
from jax.sharding import PartitionSpec as P

HD = 128
CORES = 2
BEAMS = 8
CAP = 2
PAD = 8
HIDE = -1e30
F32 = jnp.float32
BF16 = jnp.bfloat16


def iota(shape, dim):
    return lax.broadcasted_iota(jnp.int32, shape, dim)


def dot(a, b):
    return jnp.dot(a, b, preferred_element_type=F32)


def dot_last(a, b):
    return lax.dot_general(a, b, (((1,), (1,)), ((), ())), preferred_element_type=F32)


def call(kernel, outs, *args, cost=None, in_hbm=(), out_hbm=(), scratch=(), limit=16):
    flops, nbytes = cost or (0, 0)
    return pl.pallas_call(
        kernel,
        out_shape=outs,
        in_specs=[pl.BlockSpec(memory_space=pltpu.HBM if i in in_hbm else pltpu.VMEM) for i in range(len(args))],
        out_specs=[pl.BlockSpec(memory_space=pltpu.HBM if i in out_hbm else pltpu.VMEM) for i in range(len(outs))],
        scratch_shapes=scratch,
        compiler_params=pltpu.CompilerParams(vmem_limit_bytes=limit * 1024 * 1024),
        cost_estimate=pl.CostEstimate(flops=flops, bytes_accessed=nbytes, transcendentals=0),
    )(*args)


def place_of(device, parts):
    return (device + parts // 2) % parts


def copies_kernel(token_ref, out_ref):
    for i in range(out_ref.shape[0]):
        out_ref[i] = token_ref[...]


def plan_kernel(
    rows, steps, prefix, experts, first_expert,
    parents_ref, route_ref, gate_ref, bias_ref, pack_ref, high_ref, low_ref,
):
    total = rows * steps
    first = iota((rows, 1), 0) // BEAMS * BEAMS
    diagonal = iota((rows, rows), 0) == iota((rows, rows), 1)
    eye = diagonal.astype(F32)

    def column(row):
        return jnp.sum(jnp.where(iota((row.shape[1], row.shape[1]), 0) == iota((row.shape[1], row.shape[1]), 1), row, 0.0), axis=1, keepdims=True)

    parent = [
        (iota((rows, rows), 1) == first + column(parents_ref[t : t + 1, :].astype(F32)).astype(jnp.int32)).astype(F32).astype(BF16)
        for t in range(steps)
    ]
    none = jnp.zeros((rows, rows), F32)
    origin = []
    seen = []
    for t in range(steps):
        if t == 0:
            origin.append(parent[0].astype(F32))
            seen.append([eye] + [none] * (steps - 1))
        else:
            origin.append(dot(parent[t], origin[t - 1].astype(BF16)))
            seen.append([dot(parent[t], seen[t - 1][s].astype(BF16)) for s in range(t)] + [eye] + [none] * (steps - 1 - t))
    spread = (iota((rows, rows * prefix), 1) // prefix == iota((rows, rows * prefix), 0)).astype(F32).astype(BF16)
    old = dot(jnp.concatenate(origin, axis=0).astype(BF16), spread)
    bias_ref[:, : rows * prefix] = jnp.where(old > 0.5, 0.0, HIDE)
    new = jnp.concatenate([jnp.concatenate(seen[t], axis=1) for t in range(steps)], axis=0)
    bias_ref[:, rows * prefix :] = jnp.full((total, HD), HIDE, F32)
    bias_ref[:, rows * prefix : rows * prefix + total] = jnp.where(new > 0.5, 0.0, HIDE)

    a, b = iota((total, total), 0), iota((total, total), 1)
    same = a // rows == b // rows
    after = (same & (a < b)).astype(F32).astype(BF16)
    places = [
        jnp.concatenate([(route_ref[t, k : k + 1, :] + (experts - first_expert)) % experts for t in range(steps)], axis=1)
        for k in range(2)
    ]
    gates = [jnp.concatenate([gate_ref[t, k : k + 1, :] for t in range(steps)], axis=1) for k in range(2)]
    named = [(iota((experts, total), 0) == places[k]).astype(F32) for k in range(2)]
    count = dot((named[0] + named[1]).astype(BF16), after)
    step_at = (iota((1, total), 1) // rows) * CAP
    chosen = jnp.zeros((experts * PAD, total), F32)
    weights = jnp.zeros((total, experts * PAD), F32)
    for k in range(2):
        order = jnp.sum(named[k] * count, axis=0, keepdims=True).astype(jnp.int32)
        target = places[k] * PAD + step_at + order
        chosen += (iota((experts * PAD, total), 0) == target).astype(F32)
        at = column(target.astype(F32)).astype(jnp.int32)
        weights += jnp.where(iota((total, experts * PAD), 1) == at, column(gates[k]), 0.0)
    pack_ref[...] = chosen.astype(BF16)
    high = weights.astype(BF16)
    high_ref[...] = high
    low_ref[...] = (weights - high.astype(F32)).astype(BF16)


def normed_blocks(blocks):
    width = sum(v.shape[-1] for v in blocks)
    mean = sum(jnp.sum(v, axis=-1, keepdims=True) for v in blocks) / width
    centred = [v - mean for v in blocks]
    spread = sum(jnp.sum(v * v, axis=-1, keepdims=True) for v in centred) / width
    scale = lax.rsqrt(spread + 1e-05)
    return jnp.concatenate([(v * scale).astype(BF16) for v in centred], axis=-1)


def attend_kernel(prefix, gathered_ref, token_ref, w_ref, cache_ref, bias_ref, pack_ref, middle_ref, packed_ref):
    parts = gathered_ref.shape[0]
    total, shard = token_ref.shape
    rows = cache_ref.shape[0]
    normed = normed_blocks([gathered_ref[place_of(i, parts)].astype(F32) for i in range(parts)])
    query, key, value = (dot(normed, w_ref[j]).astype(BF16) for j in range(3))
    bias_old = bias_ref[:, : rows * prefix]
    bias_new = bias_ref[:, rows * prefix : rows * prefix + total]
    for h in range(shard // HD):
        at = slice(h * HD, (h + 1) * HD)
        old_keys = cache_ref[:, 0, :, at].reshape(rows * prefix, HD)
        old_values = cache_ref[:, 1, :, at].reshape(rows * prefix, HD)
        w_old = jnp.exp(dot_last(query[:, at], old_keys) * HD ** (-0.5) + bias_old)
        w_new = jnp.exp(dot_last(query[:, at], key[:, at]) * HD ** (-0.5) + bias_new)
        weight = jnp.sum(w_old, axis=-1, keepdims=True) + jnp.sum(w_new, axis=-1, keepdims=True)
        summed = dot(w_old.astype(BF16), old_values) + dot(w_new.astype(BF16), value[:, at])
        middle_ref[:, at] = (token_ref[:, at].astype(F32) + summed / weight).astype(BF16)
    packed_ref[...] = dot(pack_ref[...], middle_ref[...]).astype(BF16)


def spread_kernel(used, arrived_ref, out_ref):
    group = 8
    keep = (iota((group * used, group * PAD), 1) == (iota((group * used, 1), 0) // used) * PAD + iota((group * used, 1), 0) % used)
    keep = keep.astype(F32).astype(BF16)
    for g in range(arrived_ref.shape[0] // (group * PAD)):
        block = dot(keep, arrived_ref[g * group * PAD : (g + 1) * group * PAD, :]).astype(BF16)
        for i in range(out_ref.shape[0]):
            out_ref[i, g * group * used : (g + 1) * group * used, :] = block


def norm_kernel(slots_ref, up_hbm, normed_ref, up_ref, sem):
    copy = pltpu.make_async_copy(up_hbm, up_ref, sem)
    copy.start()
    parts, slots, _ = slots_ref.shape
    block = slots // 3
    for g in range(slots // block):
        at = slice(g * block, (g + 1) * block)
        normed_ref[at, :] = normed_blocks([slots_ref[place_of(i, parts), at, :].astype(F32) for i in range(parts)])
    copy.wait()


def own_half_kernel(normed_ref, up_ref, down_ref, sum_ref, hidden_ref):
    units, width = down_ref.shape[1:]
    wide = 256
    for n in range(0, units, wide):
        at = slice(n, n + wide)
        hidden_ref[:, at] = jax.nn.relu(dot(normed_ref[...], up_ref[0, :, at])).astype(BF16)
    for n in range(0, width, wide):
        at = slice(n, n + wide)
        sum_ref[:, at] = dot(hidden_ref[...], down_ref[0, :, at])


def other_half_kernel(normed_ref, sum_ref, up_ref, down_ref, out_ref, hidden_ref):
    units, width = down_ref.shape[1:]
    wide = width // out_ref.shape[0]
    for n in range(0, units, wide):
        at = slice(n, n + wide)
        hidden_ref[:, at] = jax.nn.relu(dot(normed_ref[...], up_ref[0, :, at])).astype(BF16)
    for i in range(out_ref.shape[0]):
        at = slice(i * wide, (i + 1) * wide)
        out_ref[place_of(i, out_ref.shape[0])] = (sum_ref[:, at] + dot(hidden_ref[...], down_ref[0, :, at])).astype(BF16)


def sum_kernel(used, parts_ref, out_ref):
    group = 8
    place = (iota((group * PAD, group * used), 0) == (iota((1, group * used), 1) // used) * PAD + iota((1, group * used), 1) % used)
    place = place.astype(F32).astype(BF16)
    for g in range(out_ref.shape[0] // (group * PAD)):
        at = slice(g * group * used, (g + 1) * group * used)
        total = sum(parts_ref[i, at, :].astype(F32) for i in range(parts_ref.shape[0]))
        out_ref[g * group * PAD : (g + 1) * group * PAD, :] = dot(place, total.astype(BF16)).astype(BF16)


def combine_kernel(middle_ref, returned_ref, high_ref, low_ref, out_ref):
    total = middle_ref.shape[0]
    both = dot(jnp.concatenate([high_ref[...], low_ref[...]], axis=0), returned_ref[...])
    added = both[:total] + both[total:]
    out_ref[...] = (middle_ref[...].astype(F32) + added).astype(BF16)


def shards(parts, experts, embeds, prefix_cache, w_qkv, w_up, w_down, parents, routes, gates):
    steps, rows, shard = embeds.shape
    width = w_qkv.shape[0]
    prefix = prefix_cache.shape[2]
    total = steps * rows
    used = steps * CAP
    slots = experts * used
    shape = jax.ShapeDtypeStruct

    first_expert = experts // 2 + 6
    order = [[(p + first_expert) % experts for p in range(experts)]]

    def exchange(values, axis):
        groups = order if axis == "yz" else [[place_of(p, parts) for p in range(parts)]]
        return lax.all_to_all(values, axis, split_axis=0, concat_axis=0, tiled=True, axis_index_groups=groups)

    tokens = embeds.reshape(total, shard)
    (copies,) = call(copies_kernel, [shape((parts, total, shard), BF16)], tokens, cost=(10**9, 10**7))
    gathered = exchange(copies, "x")
    hidden = w_up.shape[2]
    swap = [(i, (i + 1) % CORES) for i in range(CORES)]
    up_other = lax.ppermute(w_up, "core", swap)
    down_other = lax.ppermute(w_down, "core", swap)
    bias, pack, high, low = call(
        functools.partial(plan_kernel, rows, steps, prefix, experts, first_expert),
        (
            shape((total, rows * prefix + HD), F32),
            shape((experts * PAD, total), BF16),
            shape((total, experts * PAD), BF16),
            shape((total, experts * PAD), BF16),
        ),
        parents,
        routes.transpose(0, 2, 1),
        gates.transpose(0, 2, 1),
        cost=(10**9, 10**7),
    )
    middle, packed = call(
        functools.partial(attend_kernel, prefix),
        (shape((total, shard), BF16), shape((experts * PAD, shard), BF16)),
        gathered,
        tokens,
        w_qkv.transpose(1, 0, 2),
        prefix_cache,
        bias,
        pack,
        cost=(2 * total * width * 3 * shard, 3 * 10**6),
    )
    arrived = exchange(packed.reshape(experts, PAD, shard), "yz").reshape(experts * PAD, shard)
    (spread,) = call(functools.partial(spread_kernel, used), [shape((parts, slots, shard), BF16)], arrived)
    whole = exchange(spread, "x")
    normed, up_own = call(
        norm_kernel,
        [shape((slots, width), BF16), shape(w_up.shape, BF16)],
        whole,
        w_up,
        cost=(10**9, 10**7),
        in_hbm=(1,),
        scratch=[pltpu.SemaphoreType.DMA],
    )
    (half,) = call(
        own_half_kernel,
        [shape((slots, width), F32)],
        normed,
        up_own,
        w_down,
        cost=(10**11, 10**7),
        scratch=[pltpu.VMEM((slots, hidden), BF16)],
    )
    (share,) = call(
        other_half_kernel,
        [shape((parts, slots, shard), BF16)],
        normed,
        half,
        up_other,
        down_other,
        cost=(4 * slots * width * hidden, 6 * 10**6),
        scratch=[pltpu.VMEM((slots, hidden), BF16)],
    )
    pieces = exchange(share, "x")
    (summed,) = call(functools.partial(sum_kernel, used), [shape((experts * PAD, shard), BF16)], pieces)
    returned = exchange(summed.reshape(experts, PAD, shard), "yz").reshape(experts * PAD, shard)
    (mixed,) = call(combine_kernel, [shape((total, shard), BF16)], middle, returned, high, low)
    return mixed.reshape(steps, rows, shard)


def solution(mesh):
    parts, devices = mesh.shape["dp"], mesh.shape["expert"]
    experts = devices // CORES
    split = Mesh(mesh.devices.reshape(parts, experts, CORES), ("x", "yz", "core"))
    rows = ("yz", "core")
    placed = (
        P(None, rows, "x"),
        P(rows, None, None, "x"),
        P(None, None, "x"),
        P(rows, None, "x"),
        P(rows, "x", None),
        P(None, rows),
        P(None, rows, None),
        P(None, rows, None),
    )
    return jax.shard_map(
        functools.partial(shards, parts, experts), mesh=split, in_specs=placed, out_specs=P(None, rows, "x"), check_vma=False
    )
```

```python
import functools

import jax
import jax.numpy as jnp
from jax import lax
from jax.experimental import pallas as pl
from jax.experimental.pallas import tpu as pltpu
from jax.sharding import Mesh
from jax.sharding import PartitionSpec as P

HD = 128
CORES = 2
BEAMS = 8
CAP = 2
PAD = 8
HIDE = -1e30
F32 = jnp.float32
BF16 = jnp.bfloat16


def iota(shape, dim):
    return lax.broadcasted_iota(jnp.int32, shape, dim)


def dot(a, b):
    return jnp.dot(a, b, preferred_element_type=F32)


def dot_last(a, b):
    return lax.dot_general(a, b, (((1,), (1,)), ((), ())), preferred_element_type=F32)


def call(kernel, outs, *args, cost=None, in_hbm=(), out_hbm=(), scratch=(), limit=16):
    flops, nbytes = cost or (0, 0)
    return pl.pallas_call(
        kernel,
        out_shape=outs,
        in_specs=[pl.BlockSpec(memory_space=pltpu.HBM if i in in_hbm else pltpu.VMEM) for i in range(len(args))],
        out_specs=[pl.BlockSpec(memory_space=pltpu.HBM if i in out_hbm else pltpu.VMEM) for i in range(len(outs))],
        scratch_shapes=scratch,
        compiler_params=pltpu.CompilerParams(vmem_limit_bytes=limit * 1024 * 1024),
        cost_estimate=pl.CostEstimate(flops=flops, bytes_accessed=nbytes, transcendentals=0),
    )(*args)


def place_of(device, parts):
    return (device + parts // 2) % parts


def copies_kernel(token_ref, out_ref):
    for i in range(out_ref.shape[0]):
        out_ref[i] = token_ref[...]


def plan_kernel(
    rows, steps, prefix, experts, first_expert,
    parents_ref, route_ref, gate_ref, bias_ref, pack_ref, high_ref, low_ref,
):
    total = rows * steps
    first = iota((rows, 1), 0) // BEAMS * BEAMS
    diagonal = iota((rows, rows), 0) == iota((rows, rows), 1)
    eye = diagonal.astype(F32)

    def column(row):
        return jnp.sum(jnp.where(iota((row.shape[1], row.shape[1]), 0) == iota((row.shape[1], row.shape[1]), 1), row, 0.0), axis=1, keepdims=True)

    parent = [
        (iota((rows, rows), 1) == first + column(parents_ref[t : t + 1, :].astype(F32)).astype(jnp.int32)).astype(F32).astype(BF16)
        for t in range(steps)
    ]
    none = jnp.zeros((rows, rows), F32)
    origin = []
    seen = []
    for t in range(steps):
        if t == 0:
            origin.append(parent[0].astype(F32))
            seen.append([eye] + [none] * (steps - 1))
        else:
            origin.append(dot(parent[t], origin[t - 1].astype(BF16)))
            seen.append([dot(parent[t], seen[t - 1][s].astype(BF16)) for s in range(t)] + [eye] + [none] * (steps - 1 - t))
    spread = (iota((rows, rows * prefix), 1) // prefix == iota((rows, rows * prefix), 0)).astype(F32).astype(BF16)
    old = dot(jnp.concatenate(origin, axis=0).astype(BF16), spread)
    bias_ref[:, : rows * prefix] = jnp.where(old > 0.5, 0.0, HIDE)
    new = jnp.concatenate([jnp.concatenate(seen[t], axis=1) for t in range(steps)], axis=0)
    bias_ref[:, rows * prefix :] = jnp.full((total, HD), HIDE, F32)
    bias_ref[:, rows * prefix : rows * prefix + total] = jnp.where(new > 0.5, 0.0, HIDE)

    a, b = iota((total, total), 0), iota((total, total), 1)
    same = a // rows == b // rows
    after = (same & (a < b)).astype(F32).astype(BF16)
    places = [
        jnp.concatenate([(route_ref[t, k : k + 1, :] + (experts - first_expert)) % experts for t in range(steps)], axis=1)
        for k in range(2)
    ]
    gates = [jnp.concatenate([gate_ref[t, k : k + 1, :] for t in range(steps)], axis=1) for k in range(2)]
    named = [(iota((experts, total), 0) == places[k]).astype(F32) for k in range(2)]
    count = dot((named[0] + named[1]).astype(BF16), after)
    step_at = (iota((1, total), 1) // rows) * CAP
    chosen = jnp.zeros((experts * PAD, total), F32)
    weights = jnp.zeros((total, experts * PAD), F32)
    for k in range(2):
        order = jnp.sum(named[k] * count, axis=0, keepdims=True).astype(jnp.int32)
        target = places[k] * PAD + step_at + order
        chosen += (iota((experts * PAD, total), 0) == target).astype(F32)
        at = column(target.astype(F32)).astype(jnp.int32)
        weights += jnp.where(iota((total, experts * PAD), 1) == at, column(gates[k]), 0.0)
    pack_ref[...] = chosen.astype(BF16)
    high = weights.astype(BF16)
    high_ref[...] = high
    low_ref[...] = (weights - high.astype(F32)).astype(BF16)


def normed_blocks(blocks):
    width = sum(v.shape[-1] for v in blocks)
    mean = sum(jnp.sum(v, axis=-1, keepdims=True) for v in blocks) / width
    centred = [v - mean for v in blocks]
    spread = sum(jnp.sum(v * v, axis=-1, keepdims=True) for v in centred) / width
    scale = lax.rsqrt(spread + 1e-05)
    return jnp.concatenate([(v * scale).astype(BF16) for v in centred], axis=-1)


def attend_kernel(prefix, gathered_ref, token_ref, w_ref, cache_ref, bias_ref, pack_ref, middle_ref, packed_ref):
    parts = gathered_ref.shape[0]
    total, shard = token_ref.shape
    rows = cache_ref.shape[0]
    normed = normed_blocks([gathered_ref[place_of(i, parts)].astype(F32) for i in range(parts)])
    query, key, value = (dot(normed, w_ref[j]).astype(BF16) for j in range(3))
    bias_old = bias_ref[:, : rows * prefix]
    bias_new = bias_ref[:, rows * prefix : rows * prefix + total]
    for h in range(shard // HD):
        at = slice(h * HD, (h + 1) * HD)
        old_keys = cache_ref[:, 0, :, at].reshape(rows * prefix, HD)
        old_values = cache_ref[:, 1, :, at].reshape(rows * prefix, HD)
        w_old = jnp.exp(dot_last(query[:, at], old_keys) * HD ** (-0.5) + bias_old)
        w_new = jnp.exp(dot_last(query[:, at], key[:, at]) * HD ** (-0.5) + bias_new)
        weight = jnp.sum(w_old, axis=-1, keepdims=True) + jnp.sum(w_new, axis=-1, keepdims=True)
        summed = dot(w_old.astype(BF16), old_values) + dot(w_new.astype(BF16), value[:, at])
        middle_ref[:, at] = (token_ref[:, at].astype(F32) + summed / weight).astype(BF16)
    packed_ref[...] = dot(pack_ref[...], middle_ref[...]).astype(BF16)


def spread_kernel(used, arrived_ref, out_ref):
    group = 8
    keep = (iota((group * used, group * PAD), 1) == (iota((group * used, 1), 0) // used) * PAD + iota((group * used, 1), 0) % used)
    keep = keep.astype(F32).astype(BF16)
    for g in range(arrived_ref.shape[0] // (group * PAD)):
        block = dot(keep, arrived_ref[g * group * PAD : (g + 1) * group * PAD, :]).astype(BF16)
        for i in range(out_ref.shape[0]):
            out_ref[i, g * group * used : (g + 1) * group * used, :] = block


def norm_kernel(slots_ref, up_hbm, normed_ref, up_ref, sem):
    copy = pltpu.make_async_copy(up_hbm, up_ref, sem)
    copy.start()
    parts, slots, _ = slots_ref.shape
    block = slots // 3
    for g in range(slots // block):
        at = slice(g * block, (g + 1) * block)
        normed_ref[at, :] = normed_blocks([slots_ref[place_of(i, parts), at, :].astype(F32) for i in range(parts)])
    copy.wait()


def own_half_kernel(normed_ref, up_ref, down_ref, sum_ref, hidden_ref):
    units, width = down_ref.shape[1:]
    wide = 256
    for n in range(0, units, wide):
        at = slice(n, n + wide)
        hidden_ref[:, at] = jax.nn.relu(dot(normed_ref[...], up_ref[0, :, at])).astype(BF16)
    for n in range(0, width, wide):
        at = slice(n, n + wide)
        sum_ref[:, at] = dot(hidden_ref[...], down_ref[0, :, at])


def other_half_kernel(normed_ref, sum_ref, up_ref, down_ref, out_ref, hidden_ref):
    units, width = down_ref.shape[1:]
    wide = width // out_ref.shape[0]
    for n in range(0, units, wide):
        at = slice(n, n + wide)
        hidden_ref[:, at] = jax.nn.relu(dot(normed_ref[...], up_ref[0, :, at])).astype(BF16)
    for i in range(out_ref.shape[0]):
        at = slice(i * wide, (i + 1) * wide)
        out_ref[place_of(i, out_ref.shape[0])] = (sum_ref[:, at] + dot(hidden_ref[...], down_ref[0, :, at])).astype(BF16)


def sum_kernel(used, parts_ref, out_ref):
    group = 8
    place = (iota((group * PAD, group * used), 0) == (iota((1, group * used), 1) // used) * PAD + iota((1, group * used), 1) % used)
    place = place.astype(F32).astype(BF16)
    for g in range(out_ref.shape[0] // (group * PAD)):
        at = slice(g * group * used, (g + 1) * group * used)
        total = sum(parts_ref[i, at, :].astype(F32) for i in range(parts_ref.shape[0]))
        out_ref[g * group * PAD : (g + 1) * group * PAD, :] = dot(place, total.astype(BF16)).astype(BF16)


def combine_kernel(middle_ref, returned_ref, high_ref, low_ref, out_ref):
    total = middle_ref.shape[0]
    both = dot(jnp.concatenate([high_ref[...], low_ref[...]], axis=0), returned_ref[...])
    added = both[:total] + both[total:]
    out_ref[...] = (middle_ref[...].astype(F32) + added).astype(BF16)


def shards(parts, experts, embeds, prefix_cache, w_qkv, w_up, w_down, parents, routes, gates):
    steps, rows, shard = embeds.shape
    width = w_qkv.shape[0]
    prefix = prefix_cache.shape[2]
    total = steps * rows
    used = steps * CAP
    slots = experts * used
    shape = jax.ShapeDtypeStruct

    first_expert = experts // 2 + 3
    order = [[(p + first_expert) % experts for p in range(experts)]]

    def exchange(values, axis):
        groups = order if axis == "yz" else [[place_of(p, parts) for p in range(parts)]]
        return lax.all_to_all(values, axis, split_axis=0, concat_axis=0, tiled=True, axis_index_groups=groups)

    tokens = embeds.reshape(total, shard)
    (copies,) = call(copies_kernel, [shape((parts, total, shard), BF16)], tokens, cost=(10**9, 10**7))
    gathered = exchange(copies, "x")
    hidden = w_up.shape[2]
    swap = [(i, (i + 1) % CORES) for i in range(CORES)]
    up_other = lax.ppermute(w_up, "core", swap)
    down_other = lax.ppermute(w_down, "core", swap)
    bias, pack, high, low = call(
        functools.partial(plan_kernel, rows, steps, prefix, experts, first_expert),
        (
            shape((total, rows * prefix + HD), F32),
            shape((experts * PAD, total), BF16),
            shape((total, experts * PAD), BF16),
            shape((total, experts * PAD), BF16),
        ),
        parents,
        routes.transpose(0, 2, 1),
        gates.transpose(0, 2, 1),
        cost=(10**9, 10**7),
    )
    middle, packed = call(
        functools.partial(attend_kernel, prefix),
        (shape((total, shard), BF16), shape((experts * PAD, shard), BF16)),
        gathered,
        tokens,
        w_qkv.transpose(1, 0, 2),
        prefix_cache,
        bias,
        pack,
        cost=(2 * total * width * 3 * shard, 3 * 10**6),
    )
    arrived = exchange(packed.reshape(experts, PAD, shard), "yz").reshape(experts * PAD, shard)
    (spread,) = call(functools.partial(spread_kernel, used), [shape((parts, slots, shard), BF16)], arrived)
    whole = exchange(spread, "x")
    normed, up_own = call(
        norm_kernel,
        [shape((slots, width), BF16), shape(w_up.shape, BF16)],
        whole,
        w_up,
        cost=(10**9, 10**7),
        in_hbm=(1,),
        scratch=[pltpu.SemaphoreType.DMA],
    )
    (half,) = call(
        own_half_kernel,
        [shape((slots, width), F32)],
        normed,
        up_own,
        w_down,
        cost=(10**11, 10**7),
        scratch=[pltpu.VMEM((slots, hidden), BF16)],
    )
    (share,) = call(
        other_half_kernel,
        [shape((parts, slots, shard), BF16)],
        normed,
        half,
        up_other,
        down_other,
        cost=(4 * slots * width * hidden, 6 * 10**6),
        scratch=[pltpu.VMEM((slots, hidden), BF16)],
    )
    pieces = exchange(share, "x")
    (summed,) = call(functools.partial(sum_kernel, used), [shape((experts * PAD, shard), BF16)], pieces)
    returned = exchange(summed.reshape(experts, PAD, shard), "yz").reshape(experts * PAD, shard)
    (mixed,) = call(combine_kernel, [shape((total, shard), BF16)], middle, returned, high, low)
    return mixed.reshape(steps, rows, shard)


def solution(mesh):
    parts, devices = mesh.shape["dp"], mesh.shape["expert"]
    experts = devices // CORES
    split = Mesh(mesh.devices.reshape(parts, experts, CORES), ("x", "yz", "core"))
    rows = ("yz", "core")
    placed = (
        P(None, rows, "x"),
        P(rows, None, None, "x"),
        P(None, None, "x"),
        P(rows, None, "x"),
        P(rows, "x", None),
        P(None, rows),
        P(None, rows, None),
        P(None, rows, None),
    )
    return jax.shard_map(
        functools.partial(shards, parts, experts), mesh=split, in_specs=placed, out_specs=P(None, rows, "x"), check_vma=False
    )
```
